32 devices in a mesh: dp: 8 (over z, x), fsdp: 4 (over y, core).
Axes of the slice: x: 2, y: 2, z: 4, core: 2. Of those that a mesh axis runs over, the one named last changes fastest.
Arguments:
- tokens: bfloat16 [32768, 768], P(('dp', 'fsdp')), may hold values from -6 to 6
- masked_rows: int32 [32768], P(('dp', 'fsdp')), may hold values 0 or 1
- replace_ids: int32 [32768], P(('dp', 'fsdp')), may hold values from 0 to 767
- cotangent: bfloat16 [32768, 768], P(('dp', 'fsdp')), may hold values from -6 to 6
- qkv_weight: bfloat16 [768, 2304], P(None, 'fsdp'), may hold values from -0.3125 to 0.3125
- query_bias: bfloat16 [768], P('fsdp'), may hold values from -3 to 3
- value_bias: bfloat16 [768], P('fsdp'), may hold values from -3 to 3
- proj_weight: bfloat16 [768, 768], P(None, 'fsdp'), may hold values from -0.875 to 0.875
- proj_bias: bfloat16 [768], P('fsdp'), may hold values from -3 to 3
- first_gain: bfloat16 [768], P('fsdp'), may hold values from 0.5 to 1.5
- first_shift: bfloat16 [768], P('fsdp'), may hold values from -3 to 3
- inner_weight: bfloat16 [768, 3072], P(None, 'fsdp'), may hold values from -0.21875 to 0.21875
- inner_bias: bfloat16 [3072], P('fsdp'), may hold values from -3 to 3
- outer_weight: bfloat16 [3072, 768], P('fsdp'), may hold values from -0.109375 to 0.109375
- outer_bias: bfloat16 [768], P('fsdp'), may hold values from -3 to 3
- second_gain: bfloat16 [768], P('fsdp'), may hold values from 0.5 to 1.5
- second_shift: bfloat16 [768], P('fsdp'), may hold values from -3 to 3
- embed_table: bfloat16 [768, 768], P('fsdp'), may hold values from -6 to 6
Outputs:
- layer_out: bfloat16 [32768, 768], P(('dp', 'fsdp'))
- token_grad: float32 [32768, 768], P(('dp', 'fsdp'))
- qkv_weight_grad: float32 [768, 2304], P(None, 'fsdp')
- query_bias_grad: float32 [768], P('fsdp')
- value_bias_grad: float32 [768], P('fsdp')
- proj_weight_grad: float32 [768, 768], P(None, 'fsdp')
- proj_bias_grad: float32 [768], P('fsdp')
- first_gain_grad: float32 [768], P('fsdp')
- first_shift_grad: float32 [768], P('fsdp')
- inner_weight_grad: float32 [768, 3072], P(None, 'fsdp')
- inner_bias_grad: float32 [3072], P('fsdp')
- outer_weight_grad: float32 [3072, 768], P('fsdp')
- outer_bias_grad: float32 [768], P('fsdp')
- second_gain_grad: float32 [768], P('fsdp')
- second_shift_grad: float32 [768], P('fsdp')
- embed_table_grad: float32 [768, 768], P('fsdp')
The draws below stay inside these ranges and needn't reach their ends.
All inputs are finite; a program needn't handle non-finite values. No bound on the sum of `masked_rows` on one device may be relied on, other than what follows from the above.
Results may differ from the reference program's by a relative error of at most 0.023.
Values may be sent and summed in bfloat16 or wider, within the bound.
A program may use at most 192 MiB of HBM per device.

```python
import jax
import jax.numpy as jnp
from jax import lax

D = 768
HEADS = 12
HEAD = 64
FF = 3072
TABLE = 768
SEQ = 512
PAGES = 64
TOKENS = 32768


def with_ends(entries, own_key, smallest, high):
    longest = entries.shape.index(max(entries.shape))
    spots = []
    for shift in (0, 1):
        where = [jax.random.randint(jax.random.fold_in(own_key, axis), (), 0, length) for axis, length in enumerate(entries.shape)]
        where[longest] = (where[longest] + shift) % entries.shape[longest]
        spots.append(tuple(where))
    return entries.at[spots[0]].set(smallest).at[spots[1]].set(high)


def block_levels(stream_key, dims, split, least, top_value):
    level, own = 1.0, jax.random.fold_in(stream_key, 6)
    for axis_at, parts in split:
        heights = jnp.exp(jax.random.uniform(jax.random.fold_in(own, axis_at), (parts,), jnp.float32, least / len(split), top_value / len(split)))
        level = level * jnp.repeat(heights, dims[axis_at] // parts).reshape([-1 if axis == axis_at else 1 for axis in range(len(dims))])
    return level


def bell_draw(own_key, dims, deviation, bound, split=(), held_as=jnp.bfloat16):
    loudness = block_levels(own_key, dims, split, -0.22, 0.18) if split else 1.0
    values = jax.random.normal(own_key, dims, jnp.float32) * deviation * loudness
    return jnp.minimum(jnp.maximum(values, -bound), bound).astype(held_as)


def setup_inputs(seed: int = 0) -> dict:
    streams_of = jax.random.split(jax.random.key(seed), 19)
    tokens = bell_draw(streams_of[0], (TOKENS, D), 1.0, 6.0, ((0, 32),))
    masked_rows = with_ends((jax.random.randint(streams_of[1], (TOKENS,), 0, 100) < 15).astype(jnp.int32), jax.random.fold_in(streams_of[1], 1), 0, 1)
    replace_ids = with_ends(jax.random.randint(streams_of[2], (TOKENS,), 0, TABLE), jax.random.fold_in(streams_of[2], 1), 0, TABLE - 1).astype(jnp.int32)
    cotangent = bell_draw(streams_of[3], (TOKENS, D), 1.0, 6.0, ((0, 32),))
    qkv_weight = bell_draw(streams_of[4], (D, 3 * D), (D // 2) ** -0.5, 0.3125, ((1, 4),))
    query_bias = bell_draw(streams_of[5], (D,), 0.5, 3.0, ((0, 4),))
    value_bias = bell_draw(streams_of[6], (D,), 0.5, 3.0, ((0, 4),))
    proj_weight = bell_draw(streams_of[7], (D, D), (D // 16) ** -0.5, 0.875, ((1, 4),))
    proj_bias = bell_draw(streams_of[8], (D,), 0.5, 3.0, ((0, 4),))
    first_gain = jnp.clip(1.0 + 0.1 * jax.random.normal(streams_of[9], (D,), jnp.float32), 0.5, 1.5).astype(jnp.bfloat16)
    first_shift = bell_draw(streams_of[10], (D,), 0.5, 3.0, ((0, 4),))
    inner_weight = bell_draw(streams_of[11], (D, FF), D ** -0.5, 0.21875, ((1, 4),))
    inner_bias = bell_draw(streams_of[12], (FF,), 0.5, 3.0, ((0, 4),))
    outer_weight = bell_draw(streams_of[13], (FF, D), FF ** -0.5, 0.109375, ((0, 4),))
    outer_bias = bell_draw(streams_of[14], (D,), 0.5, 3.0, ((0, 4),))
    second_gain = jnp.clip(1.0 + 0.1 * jax.random.normal(streams_of[15], (D,), jnp.float32), 0.5, 1.5).astype(jnp.bfloat16)
    second_shift = bell_draw(streams_of[16], (D,), 0.5, 3.0, ((0, 4),))
    embed_table = bell_draw(streams_of[17], (TABLE, D), 1.0, 6.0, ((0, 4),))
    return {"tokens": tokens, "masked_rows": masked_rows, "replace_ids": replace_ids, "cotangent": cotangent, "qkv_weight": qkv_weight, "query_bias": query_bias, "value_bias": value_bias, "proj_weight": proj_weight, "proj_bias": proj_bias, "first_gain": first_gain, "first_shift": first_shift, "inner_weight": inner_weight, "inner_bias": inner_bias, "outer_weight": outer_weight, "outer_bias": outer_bias, "second_gain": second_gain, "second_shift": second_shift, "embed_table": embed_table}


@jax.custom_vjp
def low(v):
    return lax.optimization_barrier(v.astype(jnp.bfloat16)).astype(jnp.float32)

@jax.custom_vjp
def low_back(v):
    return v

def low_keep(v):
    return (low(v), None)

def low_pass(kept, grad):
    return (grad,)

def back_keep(v):
    return (v, None)

def back_low(kept, grad):
    return (low(grad),)
low.defvjp(low_keep, low_pass)
low_back.defvjp(back_keep, back_low)
norm_eps = 1e-05

def matmul(left, right):
    return jnp.dot(left, right, precision=lax.Precision.HIGHEST)

def norm_rows(hidden, gain, shift):
    center = lax.optimization_barrier(jnp.mean(hidden, axis=-1, keepdims=True))
    offset = hidden - center
    spread = lax.optimization_barrier(jnp.mean(offset * offset, axis=-1, keepdims=True))
    return offset * lax.rsqrt(spread + norm_eps) * gain + shift

def attend(page_qkv):
    queries = page_qkv[:, 0]
    keys = page_qkv[:, 1]
    values = page_qkv[:, 2]
    raw = low_back(jnp.einsum('qhd,khd->hqk', queries, keys, precision=lax.Precision.HIGHEST))
    scores = raw * HEAD ** (-0.5)
    largest = lax.optimization_barrier(jnp.max(scores, axis=-1, keepdims=True))
    raised = jnp.exp(scores - largest)
    probs = low_back(low(raised / lax.optimization_barrier(jnp.sum(raised, axis=-1, keepdims=True))))
    mixed = jnp.einsum('hqk,khd->qhd', probs, values, precision=lax.Precision.HIGHEST)
    return mixed.reshape(page_qkv.shape[0], D)

def layer(params, inputs, chosen, row_ids):
    qkv_weight, query_bias, value_bias, proj_weight, proj_bias, first_gain, first_shift, inner_weight, inner_bias, outer_weight, outer_bias, second_gain, second_shift, embed_table = params
    onehot = (row_ids[:, None] == jnp.arange(TABLE, dtype=jnp.int32)[None, :]).astype(jnp.float32)
    embedded = low_back(matmul(onehot, embed_table))
    start = jnp.where(chosen[:, None] > 0, embedded, inputs)
    qkv_bias = jnp.concatenate([query_bias, jnp.zeros_like(query_bias), value_bias])
    qkv = low_back(low(matmul(low(start), qkv_weight) + qkv_bias))
    pages = qkv.reshape(-1, SEQ, 3, HEADS, HEAD)
    attended = lax.map(jax.checkpoint(attend), pages).reshape(-1, D)
    attended = low_back(low(attended))
    projected = low_back(matmul(attended, proj_weight) + proj_bias)
    first = norm_rows(start + projected, first_gain, first_shift)
    inner = low_back(matmul(low(first), inner_weight) + inner_bias)
    active = low(jax.nn.gelu(inner, approximate=False))
    outer = low_back(matmul(active, outer_weight) + outer_bias)
    return norm_rows(first + outer, second_gain, second_shift)

def reference(tokens, masked_rows, replace_ids, cotangent, qkv_weight, query_bias, value_bias, proj_weight, proj_bias, first_gain, first_shift, inner_weight, inner_bias, outer_weight, outer_bias, second_gain, second_shift, embed_table):
    params = tuple((element.astype(jnp.float32) for element in (qkv_weight, query_bias, value_bias, proj_weight, proj_bias, first_gain, first_shift, inner_weight, inner_bias, outer_weight, outer_bias, second_gain, second_shift, embed_table)))
    per_group = 8 if PAGES % 8 == 0 else 1
    groups = PAGES // per_group
    width_rows = per_group * SEQ
    chosen = (masked_rows > 0).astype(jnp.float32)
    incoming = cotangent.astype(jnp.float32) * chosen[:, None]
    group_tokens = tokens.astype(jnp.float32).reshape(groups, width_rows, D)
    group_chosen = chosen.reshape(groups, width_rows)
    group_ids = replace_ids.reshape(groups, width_rows)
    group_incoming = incoming.reshape(groups, width_rows, D)

    def step(carried, inputs_all):
        these_tokens, these_chosen, these_ids, these_incoming = inputs_all

        def run(weights, inputs):
            return layer(weights, inputs, these_chosen, these_ids)
        result, pull = jax.vjp(run, params, these_tokens)
        grad_weights, grad_tokens = pull(these_incoming)
        carried = jax.tree.map(jnp.add, carried, grad_weights)
        return (carried, (result.astype(jnp.bfloat16), grad_tokens))
    zeros = tuple((jnp.zeros_like(element) for element in params))
    summed, (results, token_grads) = lax.scan(step, zeros, (group_tokens, group_chosen, group_ids, group_incoming))
    return (results.reshape(TOKENS, D), token_grads.reshape(TOKENS, D), summed[0], summed[1], summed[2], summed[3], summed[4], summed[5], summed[6], summed[7], summed[8], summed[9], summed[10], summed[11], summed[12], summed[13])
```

```python
import functools
from functools import partial

import jax
import jax.numpy as jnp
from jax import lax
from jax.experimental import pallas as pl
from jax.experimental.pallas import tpu as pltpu
from jax.sharding import PartitionSpec as P


SEQ, HEAD, HEADS, D, TABLE = 512, 64, 12, 768, 768
EPS = 1e-5
LOG2E = 1.4426950408889634
F32, BF16 = jnp.float32, jnp.bfloat16

def mm(a, b):
    return lax.dot_general(a, b, (((1,), (0,)), ((), ())), preferred_element_type=F32)

def mm_nt(a, b):
    return lax.dot_general(a, b, (((1,), (1,)), ((), ())), preferred_element_type=F32)

def upper_tail(size):
    t = pl.reciprocal(1.0 + (0.3275911 * 0.7071067811865476) * size, approx=True)
    bell = jnp.exp2(size * size * (-0.5 * LOG2E))
    poly = t * (0.127414796 + t * (-0.142248368 + t * (0.7107068705 + t * (-0.7265760135 + t * 0.5307027145))))
    return poly * bell, bell

def norm_parts(hidden):
    center = jnp.mean(hidden, axis=-1, keepdims=True)
    offset = hidden - center
    spread = jnp.mean(offset * offset, axis=-1, keepdims=True)
    inv = lax.rsqrt(spread + EPS)
    return offset * inv, inv

def row_of(vec_ref, k):
    n = vec_ref.shape[0]
    total = vec_ref[0, k:k + 1, :].astype(F32)
    for s in range(1, n):
        total = total + vec_ref[s, k:k + 1, :].astype(F32)
    return total

def embed_rows(ids_ref, tokens_ref, tab_ref, start_ref):
    lanes = lax.broadcasted_iota(jnp.int32, (128, 128), 1).astype(F32)
    def step(i, _):
        ids = jnp.broadcast_to(ids_ref[pl.ds(i, 1), :], (128, 128)).T
        hot = jnp.concatenate([(ids == lanes + 128.0 * j).astype(F32).astype(BF16) for j in range(TABLE // 128)], axis=1)
        rows = pl.ds(pl.multiple_of(i * 128, 128), 128)
        emb = mm(hot, tab_ref[...])
        kept = jnp.concatenate([ids] * (D // 128), axis=1) < 0.0
        start_ref[rows, :] = jnp.where(kept, tokens_ref[rows, :].astype(F32), emb).astype(BF16)
        return 0
    lax.fori_loop(0, ids_ref.shape[0], step, 0)

def make_colbias(vec_ref, colb_ref):
    for part, k in ((0, 1), (1, None), (2, 2)):
        row = None if k is None else row_of(vec_ref, k)
        for j in range(D // 128):
            tile = jnp.zeros((128, 128), F32) if k is None else jnp.broadcast_to(row[:, 128 * j:128 * j + 128], (128, 128)).T
            colb_ref[part * D + 128 * j:part * D + 128 * j + 128, :] = tile

def qkv_rows(o, size, wt_ref, start_ref, colb_ref, qkvt_ref):
    rows = pl.ds(pl.multiple_of(o, 64), size)
    tokens = start_ref.shape[0]
    acc = mm_nt(wt_ref[rows, :], start_ref[...])
    bias = jnp.concatenate([colb_ref[rows, :]] * (tokens // 128), axis=1)
    qkvt_ref[rows, :] = (acc + bias).astype(BF16)

def attend_pair(page, pair, qkvt_ref, att_ref):
    cols = pl.ds(pl.multiple_of(page * SEQ, SEQ), SEQ)
    ones = jnp.ones((16, SEQ), BF16)
    outs = []
    for sub in range(2):
        head = pair * 2 + sub
        at = lambda part: pl.ds(pl.multiple_of(part * D + head * HEAD, HEAD), HEAD)
        qt = qkvt_ref[at(0), cols]
        kn = qkvt_ref[at(1), cols].T
        vt = jnp.concatenate([qkvt_ref[at(2), cols], ones], axis=0)
        halves = []
        for c in range(2):
            s = mm(kn, qt[:, 256 * c:256 * c + 256])
            top = jnp.max(s, axis=0, keepdims=True)
            e = jnp.exp2((s - top) * (LOG2E * HEAD ** -0.5)).astype(BF16)
            o = mm(vt, e)
            halves.append(o[:HEAD] / o[HEAD:HEAD + 1])
        outs.append(jnp.concatenate(halves, axis=1))
    both = jnp.concatenate(outs, axis=0)
    att_ref[cols, pl.ds(pl.multiple_of(pair * 128, 128), 128)] = both.T.astype(BF16)

def proj_norm(i, size, att_ref, wpt_ref, start_ref, vec_ref, first_ref, low_ref):
    rows = pl.ds(pl.multiple_of(i * size, size), size)
    h = start_ref[rows, :].astype(F32) + (mm_nt(att_ref[rows, :], wpt_ref[...]) + row_of(vec_ref, 3))
    xhat, _ = norm_parts(h)
    first = xhat * row_of(vec_ref, 4) + row_of(vec_ref, 5)
    low_ref[rows, :] = first.astype(BF16)
    first_ref[rows, :] = first + row_of(vec_ref, 6)

def ff_part(s, i, size, low_ref, w1_ref, w2_ref, vec_ref, acc_ref):
    rows = pl.ds(pl.multiple_of(i * size, size), size)
    x = mm(low_ref[rows, :], w1_ref[s]) + vec_ref[s, 0:1, :].astype(F32)
    a = jnp.abs(x)
    q, _ = upper_tail(a)
    active = (jnp.maximum(x, 0.0) - a * q).astype(BF16)
    acc_ref[rows, :] += mm(active, w2_ref[s])

def out_norm(i, size, acc_ref, vec_ref, out_ref):
    rows = pl.ds(pl.multiple_of(i * size, size), size)
    xhat, _ = norm_parts(acc_ref[rows, :])
    out_ref[rows, :] = (xhat * row_of(vec_ref, 7) + row_of(vec_ref, 8)).astype(BF16)

def fwd_kernel(tokens, idf, tab, wt, wpt, w1, w2, vec, out, start, att, qkvt, colb, acc, low):
    T = tokens.shape[0]
    pages = T // SEQ
    make_colbias(vec, colb)
    embed_rows(idf, tokens, tab, start)
    @pl.loop(0, 9)
    def _(o):
        qkv_rows(o * 256, 256, wt, start, colb, qkvt)
    @pl.loop(0, pages * 6)
    def _(it):
        attend_pair(it // 6, it % 6, qkvt, att)
    @pl.loop(0, T // 256)
    def _(i):
        proj_norm(i, 256, att, wpt, start, vec, acc, low)
    @pl.loop(0, 4 * (T // 512))
    def _(it):
        ff_part(it // (T // 512), it % (T // 512), 512, low, w1, w2, vec, acc)
    @pl.loop(0, T // 256)
    def _(i):
        out_norm(i, 256, acc, vec, out)

def forward_call(tokens, idf, tab, wt, wpt, w1, w2, vec):
    T = tokens.shape[0]
    vm = pl.BlockSpec(memory_space=pltpu.VMEM)
    return pl.pallas_call(
        fwd_kernel,
        out_shape=[jax.ShapeDtypeStruct((T, D), BF16), jax.ShapeDtypeStruct((T, D), BF16), jax.ShapeDtypeStruct((T, D), BF16), jax.ShapeDtypeStruct((3 * D, T), BF16)],
        in_specs=[vm] * 8, out_specs=[vm] * 4,
        scratch_shapes=[pltpu.VMEM((3 * D, 128), F32), pltpu.VMEM((T, D), F32), pltpu.VMEM((T, D), BF16)],
        compiler_params=pltpu.CompilerParams(vmem_limit_bytes=60 * 2**20), name="forward",
    )(tokens, idf, tab, wt, wpt, w1, w2, vec)


ROWS_OUTER, ROWS_INNER, ROWS_PROJ, ROWS_QKV, ROWS_TABLE, ROWS_VEC = 0, 768, 1536, 1728, 2304, 2496
ROWS = 2560
HALF = 128

def mm_tn(a, b):
    return mm(a.T, b)

def norm_back(xhat, inv, gain, g):
    gx = g * gain
    return inv * (gx - jnp.mean(gx, axis=-1, keepdims=True) - xhat * jnp.mean(gx * xhat, axis=-1, keepdims=True))

def put(ref, index, value, first):
    if first:
        ref[index] = value.astype(ref.dtype)
    else:
        ref[index] = (ref[index].astype(F32) + value).astype(ref.dtype)

def bwd_kernel(nb_ref, idf, start_h, att_h, cot_h, qkvt_h, wt_h, wpt_h, w1_h, w2_h, vec_h, grad_h, token_h,
               start, att, cot, qkvt, wpt, w1, w2, vec, grad, tok,
               active, slope, low, acc, xhat_one, g_first, qct, gact, gone, gqc, gkv, gall, sums, pick, rank, sem_in, sem_out):
    T = start.shape[0]
    pages = T // SEQ
    W = pages * HALF
    arrivals = {}
    for k, (name, src, dst) in enumerate((("vec", vec_h, vec), ("start", start_h, start), ("att", att_h, att), ("wpt", wpt_h, wpt), ("w1", w1_h, w1), ("w2", w2_h, w2),
                                          ("cot", cot_h, cot), ("qkvt", qkvt_h, qkvt))):
        arrivals[name] = pltpu.make_async_copy(src, dst, sem_in.at[k])
        arrivals[name].start()

    r_i = lax.broadcasted_iota(jnp.int32, (SEQ, SEQ), 0)
    c_i = lax.broadcasted_iota(jnp.int32, (SEQ, SEQ), 1)
    upper = (r_i < c_i).astype(F32).astype(BF16)
    per = SEQ // 128
    for p in range(pages):
        ids = jnp.concatenate([idf[per * p + k:per * p + k + 1, :] for k in range(per)], axis=1)
        ids8 = jnp.broadcast_to(ids, (8, SEQ))
        hit = (ids8 >= 0.0).astype(F32)
        before = mm(jnp.concatenate([hit, hit], axis=0).astype(BF16), upper)[:8]
        rank[p] = jnp.where(ids8 >= 0.0, before, -1e6)

    sums[...] = jnp.zeros_like(sums)
    row_j = lax.broadcasted_iota(jnp.int32, (HALF, SEQ), 0).astype(F32)

    def make_pick(b):
        for p in range(pages):
            want = row_j + (b * HALF).astype(F32) if not isinstance(b, int) else row_j + float(b * HALF)
            pick[p] = (jnp.broadcast_to(rank[p][0:1, :], (HALF, SEQ)) == want).astype(F32).astype(BF16)

    def picked(ref):
        return jnp.concatenate([mm(pick[p], ref[p * SEQ:(p + 1) * SEQ, :]) for p in range(pages)], axis=0)

    def block(b, first):
        wait = (lambda n: arrivals[n].wait()) if first else (lambda n: None)
        make_pick(b)
        wait("start"); wait("att"); wait("vec"); wait("wpt")
        start_c = picked(start)
        att_c = picked(att).astype(BF16)
        h = start_c + (mm_nt(att_c, wpt[...]) + row_of(vec, 3))
        xhat, inv_one = norm_parts(h)
        xhat_one[...] = xhat
        f = xhat * row_of(vec, 4) + row_of(vec, 5)
        low[...] = f.astype(BF16)
        acc[...] = f + row_of(vec, 6)
        wait("w1"); wait("w2")
        @pl.loop(0, 4)
        def _(s):
            x = mm(low[...], w1[s]) + vec[s, 0:1, :].astype(F32)
            a = jnp.abs(x)
            q, bell = upper_tail(a)
            active[s] = (jnp.maximum(x, 0.0) - a * q).astype(BF16)
            slope[s] = (jnp.where(x >= 0.0, 1.0 - q, q) + x * (bell * 0.3989422804014327)).astype(BF16)
            acc[...] += mm(active[s], w2[s])
        xhat_two, inv_two = norm_parts(acc[...])
        wait("cot")
        g_out = picked(cot)
        sums[9:10, :] += jnp.sum(g_out * xhat_two, axis=0, keepdims=True)
        sums[10:11, :] += jnp.sum(g_out, axis=0, keepdims=True)
        g_two = norm_back(xhat_two, inv_two, row_of(vec, 7), g_out)
        g_outer = g_two.astype(BF16)
        sums[8:9, :] += jnp.sum(g_outer.astype(F32), axis=0, keepdims=True)
        g_first[...] = g_two
        low_t = low[...].T
        @pl.loop(0, 4)
        def _(s):
            put(grad, (s, pl.ds(ROWS_OUTER, D)), mm_tn(active[s], g_outer), first)
            g_inner = (mm_nt(g_outer, w2[s]) * slope[s].astype(F32)).astype(BF16)
            sums[pl.ds(s, 1), :] += jnp.sum(g_inner.astype(F32), axis=0, keepdims=True)
            put(grad, (s, pl.ds(ROWS_INNER, D)), mm(low_t, g_inner), first)
            g_first[...] += mm_nt(g_inner, w1[s])
        g = g_first[...]
        xhat = xhat_one[...]
        sums[6:7, :] += jnp.sum(g * xhat, axis=0, keepdims=True)
        sums[7:8, :] += jnp.sum(g, axis=0, keepdims=True)
        g_one = norm_back(xhat, inv_one, row_of(vec, 4), g)
        gone[b] = g_one
        g_proj = g_one.astype(BF16)
        sums[5:6, :] += jnp.sum(g_proj.astype(F32), axis=0, keepdims=True)
        dwp = mm_tn(g_proj, att_c)
        for s in range(4):
            put(grad, (s, pl.ds(ROWS_PROJ, 192)), dwp[192 * s:192 * s + 192], first)
        gact[...] = mm(g_proj, wpt[...]).astype(BF16).T
        wait("qkvt")
        for p in range(pages):
            qct[:, p * HALF:(p + 1) * HALF] = mm_nt(qkvt[0:D, p * SEQ:(p + 1) * SEQ], pick[p]).astype(BF16)
        @pl.loop(0, pages * 6)
        def _(it):
            page, pair = it // 6, it % 6
            cols = pl.ds(pl.multiple_of(page * SEQ, SEQ), SEQ)
            small = pl.ds(pl.multiple_of(page * HALF, HALF), HALF)
            for sub in range(2):
                head = pair * 2 + sub
                at = lambda part: pl.ds(pl.multiple_of(part * D + head * HEAD, HEAD), HEAD)
                kt = qkvt[at(1), cols]
                vn = qkvt[at(2), cols].T
                qt = qct[at(0), small]
                ga = gact[at(0), small]
                s = mm(kt.T, qt)
                top = jnp.max(s, axis=0, keepdims=True)
                e = jnp.exp2((s - top) * (LOG2E * HEAD ** -0.5))
                p = e * (1.0 / jnp.sum(e, axis=0, keepdims=True))
                gp = mm(vn, ga)
                d = jnp.sum(p * gp, axis=0, keepdims=True)
                gs = (p * (gp - d) * HEAD ** -0.5).astype(BF16)
                gqc[b, at(0), small] = mm(kt, gs).astype(BF16)
                put(gkv, (at(0), cols), mm_nt(qt, gs), first)
                put(gkv, (at(1), cols), mm_nt(ga, p.astype(BF16)), first)
        dwq = mm(gqc[b], start_c.astype(BF16))
        put(grad, (0, pl.ds(ROWS_QKV, 576)), dwq[:576], first)
        put(grad, (1, pl.ds(ROWS_QKV, 192)), dwq[576:], first)
        ones = jnp.ones((16, W), BF16)
        sums[4:5, :] += mm_nt(ones, gqc[b])[0:1]

    def table_block(b, first):
        make_pick(b)
        gall[0:D, :] = gqc[b]
        hots = []
        for p in range(pages):
            gall[D:3 * D, p * HALF:(p + 1) * HALF] = mm_nt(gkv[:, p * SEQ:(p + 1) * SEQ], pick[p]).astype(BF16)
            ids = jnp.concatenate([idf[per * p + k:per * p + k + 1, :] for k in range(per)], axis=1)
            hot = (jnp.broadcast_to(ids, (TABLE, SEQ)) == lax.broadcasted_iota(jnp.int32, (TABLE, SEQ), 0).astype(F32)).astype(F32).astype(BF16)
            hots.append(mm_nt(hot, pick[p]).astype(BF16))
        gt = gall[...].T
        g_start = gone[b] + sum(mm(gt[:, D * k:D * k + D], w2[k]) for k in range(3))
        dtab = mm(jnp.concatenate(hots, axis=1), g_start.astype(BF16))
        for s in range(4):
            put(grad, (s, pl.ds(ROWS_TABLE, 192)), dtab[192 * s:192 * s + 192], first)

    nb = nb_ref[0]
    block(0, True)
    @pl.loop(1, nb)
    def _(b):
        block(b, False)
    outs = []
    def send(k, src, dst):
        c = pltpu.make_async_copy(src, dst, sem_out.at[k]); c.start(); outs.append(c)
    for s in range(4):
        send(s, grad.at[s, pl.ds(0, ROWS_QKV)], grad_h.at[s, pl.ds(0, ROWS_QKV)])
    wt_copy = pltpu.make_async_copy(wt_h, w2.at[pl.ds(0, 3)], sem_in.at[8])
    wt_copy.start()
    @pl.loop(0, 8)
    def _(i):
        o = 192 * i
        at = D + o
        grad[at // 576, pl.ds(pl.multiple_of(ROWS_QKV + at % 576, 64), 192)] = mm(gkv[pl.ds(pl.multiple_of(o, 64), 192), :], start[...]).astype(BF16)
    sums[11:12, :] += mm_nt(jnp.ones((16, T), BF16), gkv[D:2 * D, :])[0:1]
    wt_copy.wait()
    table_block(0, True)
    @pl.loop(1, nb)
    def _(b):
        table_block(b, False)
    for s in range(4):
        rest = jnp.concatenate([sums[4:12, :], jnp.zeros((7, D), F32)], axis=0)
        grad[s, ROWS_VEC:ROWS_VEC + 16, :] = jnp.concatenate([sums[s:s + 1, :], rest], axis=0).astype(BF16)
        grad[s, ROWS_VEC + 16:ROWS, :] = jnp.zeros((ROWS - ROWS_VEC - 16, D), BF16)
        send(4 + s, grad.at[s, pl.ds(ROWS_QKV, ROWS - ROWS_QKV)], grad_h.at[s, pl.ds(ROWS_QKV, ROWS - ROWS_QKV)])
    @pl.loop(0, T // 256)
    def _(i):
        rows = pl.ds(pl.multiple_of(i * 256, 256), 256)
        gt = gkv[:, rows].T
        g = mm(gt[:, :D], w2[1]) + mm(gt[:, D:], w2[2])
        slot = i % 2
        @pl.when(i >= 2)
        def _():
            pltpu.make_async_copy(tok.at[slot], token_h.at[pl.ds(pl.multiple_of(i * 256 - 512, 256), 256)], sem_out.at[8 + slot]).wait()
        for k in range(2):
            ids = jnp.broadcast_to(idf[pl.ds(2 * i + k, 1), :], (128, 128)).T
            kept = jnp.concatenate([ids] * (D // 128), axis=1) < 0.0
            tok[slot, 128 * k:128 * k + 128, :] = jnp.where(kept, g[128 * k:128 * k + 128], 0.0)
        pltpu.make_async_copy(tok.at[slot], token_h.at[rows], sem_out.at[8 + slot]).start()
    for c in outs: c.wait()
    for i in range(T // 256 - 2, T // 256):
        pltpu.make_async_copy(tok.at[i % 2], token_h.at[pl.ds(256 * i, 256)], sem_out.at[8 + i % 2]).wait()

def backward_call(nb, idf, start, att, cot, qkvt, wt, wpt, w1, w2, vec):
    T = start.shape[0]
    pages = T // SEQ
    W = pages * HALF
    n = w1.shape[0]
    top = SEQ // HALF
    vm = pl.BlockSpec(memory_space=pltpu.VMEM)
    hb = pl.BlockSpec(memory_space=pl.ANY)
    same = lambda a: pltpu.VMEM(a.shape, a.dtype)
    return pl.pallas_call(
        bwd_kernel,
        out_shape=[jax.ShapeDtypeStruct((n, ROWS, D), BF16), jax.ShapeDtypeStruct((T, D), F32)],
        in_specs=[pl.BlockSpec(memory_space=pltpu.SMEM), vm] + [hb] * 9, out_specs=[hb] * 2,
        scratch_shapes=[same(a) for a in (start, att, cot, qkvt, wpt, w1, w2, vec)] + [
            pltpu.VMEM((n, ROWS, D), BF16), pltpu.VMEM((2, 256, D), F32),
            pltpu.VMEM((n, W, D), BF16), pltpu.VMEM((n, W, D), BF16), pltpu.VMEM((W, D), BF16), pltpu.VMEM((W, D), F32), pltpu.VMEM((W, D), F32), pltpu.VMEM((W, D), F32),
            pltpu.VMEM((D, W), BF16), pltpu.VMEM((D, W), BF16), pltpu.VMEM((top, W, D), F32), pltpu.VMEM((top, D, W), BF16),
            pltpu.VMEM((2 * D, T), BF16), pltpu.VMEM((3 * D, W), BF16), pltpu.VMEM((16, D), F32), pltpu.VMEM((pages, HALF, SEQ), BF16), pltpu.VMEM((pages, 8, SEQ), F32),
            pltpu.SemaphoreType.DMA((9,)), pltpu.SemaphoreType.DMA((10,))],
        compiler_params=pltpu.CompilerParams(vmem_limit_bytes=62 * 2**20), name="backward",
    )(nb, idf, start, att, cot, qkvt, wt.reshape(3, D, D), wpt, w1, w2, vec)


MESH = pl.DeviceIdType.MESH
CHUNK = 64
LAGS = (0, 2, 4, 6, 8, 10, 12)

def reduce_kernel(grad, fin_h, own, rc, sy, ry, kx, sx, rx, kz, sz, rz, se, re, fin, send_sem, recv_sem, own_sem, out_sem):
    dp, fs = lax.axis_index("dp"), lax.axis_index("fsdp")
    y, c = fs // 2, fs % 2
    x, za, zb = dp % 2, (dp // 2) % 2, dp // 4
    to_c = (dp, 2 * y + 1 - c)
    to_y = (dp, 2 * (1 - y) + c)
    to_x = (dp + 1 - 2 * x, fs)
    to_a = (dp + 2 - 4 * za, fs)
    to_b = (dp + 4 - 8 * zb, fs)
    barrier = pltpu.get_barrier_semaphore()
    for to in (to_c, to_y, to_x, to_a, to_b):
        pl.semaphore_signal(barrier, inc=1, device_id=to, device_id_type=MESH)
    pl.semaphore_wait(barrier, 5)
    n = own.shape[1] // CHUNK
    H, Q = CHUNK // 2, CHUNK // 4
    rows = lambda k: pl.ds(pl.multiple_of(k * CHUNK, CHUNK), CHUNK)
    half = lambda k, s: pl.ds(pl.multiple_of(k * CHUNK + s * H, H), H)
    quarter = lambda k, s, t: pl.ds(pl.multiple_of(k * CHUNK + s * H + t * Q, Q), Q)
    hrows = lambda k: pl.ds(pl.multiple_of(k * H, H), H)
    qrows = lambda k: pl.ds(pl.multiple_of(k * Q, Q), Q)
    f = lambda v: v.astype(F32)

    def remote(stage, k, src, dst, to):
        return pltpu.make_async_remote_copy(src_ref=src, dst_ref=dst, send_sem=send_sem.at[stage, k], recv_sem=recv_sem.at[stage, k], device_id=to, device_id_type=MESH)
    copies = [
        lambda k: remote(0, k, grad.at[:, 1 - c, rows(k), :], rc.at[:, rows(k), :], to_c),
        lambda k: remote(1, k, sy.at[rows(k)], ry.at[rows(k)], to_y),
        lambda k: remote(2, k, sx.at[hrows(k)], rx.at[hrows(k)], to_x),
        lambda k: remote(3, k, sz.at[qrows(k)], rz.at[qrows(k)], to_a),
        lambda k: remote(4, k, se.at[qrows(k)], re.at[qrows(k)], to_b),
        lambda k: remote(5, k, fin.at[quarter(k, x, za)], fin.at[quarter(k, x, za)], to_a),
        lambda k: remote(6, k, fin.at[half(k, x)], fin.at[half(k, x)], to_x),
    ]
    local = lambda k: pltpu.make_async_copy(grad.at[:, c, rows(k), :], own.at[:, rows(k), :], own_sem.at[k])
    leave = lambda k: pltpu.make_async_copy(fin.at[rows(k)], fin_h.at[rows(k)], out_sem.at[k])

    @pl.loop(0, n)
    def _(k):
        copies[0](k).start()
        local(k).start()

    def on_y(k):
        copies[0](k).wait_recv()
        local(k).wait()
        sy[rows(k), :] = (f(own[1 - y, rows(k), :]) + f(rc[1 - y, rows(k), :])).astype(BF16)
        copies[1](k).start()

    def on_x(k):
        copies[1](k).wait_recv()
        part = lambda s: f(own[y, half(k, s), :]) + f(rc[y, half(k, s), :]) + f(ry[half(k, s), :])
        sx[hrows(k), :] = part(1 - x).astype(BF16)
        copies[2](k).start()
        kx[hrows(k), :] = part(x)

    def on_a(k):
        copies[2](k).wait_recv()
        part = lambda t: kx[pl.ds(pl.multiple_of(k * H + t * Q, Q), Q), :] + f(rx[pl.ds(pl.multiple_of(k * H + t * Q, Q), Q), :])
        sz[qrows(k), :] = part(1 - za).astype(BF16)
        copies[3](k).start()
        kz[qrows(k), :] = part(za)

    def on_b(k):
        copies[3](k).wait_recv()
        se[qrows(k), :] = (kz[qrows(k), :] + f(rz[qrows(k), :])).astype(BF16)
        copies[4](k).start()

    def back_a(k):
        copies[4](k).wait_recv()
        fin[quarter(k, x, za), :] = (f(se[qrows(k), :]) + f(re[qrows(k), :])).astype(BF16)
        copies[5](k).start()

    def back_x(k):
        copies[5](k).wait_recv()
        copies[6](k).start()

    def done(k):
        copies[6](k).wait_recv()
        leave(k).start()

    @pl.loop(0, n + LAGS[-1])
    def _(t):
        for stage, lag in zip((on_y, on_x, on_a, on_b, back_a, back_x, done), LAGS):
            k = t - lag
            @pl.when((k >= 0) & (k < n))
            def _():
                stage(k)

    @pl.loop(0, n)
    def _(k):
        for copy in copies:
            copy(k).wait_send()
        leave(k).wait()

def reduce_call(grad):
    R = grad.shape[1]
    n = R // CHUNK
    hb = pl.BlockSpec(memory_space=pl.ANY)
    low = lambda *s: pltpu.VMEM(s + (D,), BF16)
    return pl.pallas_call(
        reduce_kernel,
        out_shape=jax.ShapeDtypeStruct((R, D), BF16),
        in_specs=[hb], out_specs=hb,
        scratch_shapes=[low(2, R), low(2, R), low(R), low(R), pltpu.VMEM((R // 2, D), F32), low(R // 2), low(R // 2),
                        pltpu.VMEM((R // 4, D), F32), low(R // 4), low(R // 4), low(R // 4), low(R // 4), low(R),
                        pltpu.SemaphoreType.DMA((7, n)), pltpu.SemaphoreType.DMA((7, n)), pltpu.SemaphoreType.DMA((n,)), pltpu.SemaphoreType.DMA((n,))],
        compiler_params=pltpu.CompilerParams(collective_id=1, has_side_effects=True, vmem_limit_bytes=60 * 2**20), name="reduce",
    )(grad.reshape(2, 2, R, D))

def finish_kernel(fin, outer, inner, qkv, proj, table, inner_b, *smalls):
    outer[...] = fin[ROWS_OUTER:ROWS_INNER].astype(F32)
    inner[...] = fin[ROWS_INNER:ROWS_PROJ].astype(F32)
    table[...] = fin[ROWS_TABLE:ROWS_VEC].astype(F32)
    proj[...] = fin[ROWS_PROJ:ROWS_QKV].astype(F32).T
    qkv[...] = fin[ROWS_QKV:ROWS_TABLE].astype(F32).T
    rows = fin[ROWS_VEC:ROWS_VEC + 16].astype(F32)
    inner_b[...] = rows[0]
    me = lax.axis_index("fsdp")
    part = D // lax.axis_size("fsdp")
    for k, ref in enumerate(smalls):
        ref[...] = sum(jnp.where(me == s, rows[1 + k, part * s:part * s + part], 0.0) for s in range(D // part))

def finish_call(fin):
    vm = pl.BlockSpec(memory_space=pltpu.VMEM)
    part = D // lax.axis_size("fsdp")
    shp = lambda *s: jax.ShapeDtypeStruct(s, F32)
    out = pl.pallas_call(
        finish_kernel, out_shape=[shp(D, D), shp(D, D), shp(D, 3 * part), shp(D, part), shp(part, D), shp(D)] + [shp(part)] * 8,
        in_specs=[vm], out_specs=[vm] * 14, compiler_params=pltpu.CompilerParams(vmem_limit_bytes=40 * 2**20), name="finish")(fin)
    return *out[:6], out[6:]

def local_direct(tokens, masked_rows, replace_ids, cotangent, qkv_weight, query_bias, value_bias, proj_weight, proj_bias, first_gain, first_shift,
                 inner_weight, inner_bias, outer_weight, outer_bias, second_gain, second_shift, embed_table):
    n, me = lax.axis_size("fsdp"), lax.axis_index("fsdp")
    gather = lambda v: lax.all_gather(v, "fsdp", axis=0, tiled=True)
    mine = jnp.arange(D) // (D // n) == me
    place = lambda v: jnp.where(mine, jnp.tile(v, n), 0).astype(BF16)
    smalls = (query_bias, value_bias, proj_bias, first_gain, first_shift, outer_bias, second_gain, second_shift)
    vec = jnp.stack([inner_bias] + [place(v) for v in smalls] + [jnp.zeros(D, BF16)] * 7)
    tab, wt, wpt = gather(embed_table), gather(qkv_weight.T), gather(proj_weight.T)
    w1, w2, vec = gather(inner_weight[None]), gather(outer_weight[None]), gather(vec[None])
    idf = jnp.where(masked_rows > 0, replace_ids, -1).astype(F32).reshape(-1, 128)
    out, start, att, qkvt = forward_call(tokens, idf, tab, wt, wpt, w1, w2, vec)
    blocks = jnp.max((jnp.sum(masked_rows.reshape(-1, SEQ), axis=1) + HALF - 1) // HALF)[None]
    grad, token_grad = backward_call(blocks, idf, start, att, cotangent, qkvt, wt, wpt, w1, w2, vec)
    outer, inner, qkv, proj, table, inner_b, smalls = finish_call(reduce_call(grad))
    q, pb, fg, fs, ob, sg, ss, v = smalls
    return (out, token_grad, qkv, q, v, proj, pb, fg, fs, inner, inner_b, outer, ob, sg, ss, table)


def plain_norm_rows(hidden, gain, shift):
    center = jnp.mean(hidden, axis=-1, keepdims=True)
    offset = hidden - center
    spread = jnp.mean(offset * offset, axis=-1, keepdims=True)
    return offset * lax.rsqrt(spread + EPS) * gain + shift


def plain_norm_back(hidden, gain, shift, incoming):
    _, pull = jax.vjp(plain_norm_rows, hidden, gain.astype(jnp.float32), shift.astype(jnp.float32))
    return pull(incoming)


def attend(page_qkv):
    queries = page_qkv[:, 0]
    keys = page_qkv[:, 1]
    values = page_qkv[:, 2]
    scores = jnp.einsum(
        "qhd,khd->hqk", queries, keys, preferred_element_type=jnp.float32
    ) * HEAD ** (-0.5)
    largest = jnp.max(scores, axis=-1, keepdims=True)
    raised = jnp.exp(scores - largest)
    expsum = jnp.sum(raised, axis=-1, keepdims=True)
    probs = (raised / expsum).astype(jnp.bfloat16)
    mixed = jnp.einsum("hqk,khd->qhd", probs, values, preferred_element_type=jnp.float32)
    return (mixed.reshape(page_qkv.shape[0], D), (largest + jnp.log(expsum))[..., 0])


def attend_back(inputs_all):
    page_qkv, logsum, page_grad = inputs_all
    queries = page_qkv[:, 0]
    keys = page_qkv[:, 1]
    values = page_qkv[:, 2]
    scale = HEAD ** (-0.5)
    scores = jnp.einsum("qhd,khd->hqk", queries, keys, preferred_element_type=jnp.float32) * scale
    probs = jnp.exp(scores - logsum[..., None])
    probs_low = probs.astype(jnp.bfloat16)
    grad_prob = jnp.einsum("qhd,khd->hqk", page_grad, values, preferred_element_type=jnp.float32)
    grad_prob = lax.optimization_barrier(grad_prob.astype(jnp.bfloat16)).astype(jnp.float32)
    center = jnp.sum(probs * grad_prob, axis=-1, keepdims=True)
    grad_raw = (scale * probs * (grad_prob - center)).astype(jnp.bfloat16)
    grad_query = jnp.einsum("hqk,khd->qhd", grad_raw, keys, preferred_element_type=jnp.float32)
    grad_key = jnp.einsum("hqk,qhd->khd", grad_raw, queries, preferred_element_type=jnp.float32)
    grad_value = jnp.einsum(
        "hqk,qhd->khd", probs_low, page_grad, preferred_element_type=jnp.float32
    )
    stacked = jnp.stack([grad_query, grad_key, grad_value], axis=1)
    return stacked.reshape(page_qkv.shape[0], 3 * D)


def plain_forward(weights, tokens, chosen, onehot):
    (
        qkv_weight,
        query_bias,
        value_bias,
        proj_weight,
        proj_bias,
        first_gain,
        first_shift,
        inner_weight,
        inner_bias,
        outer_weight,
        outer_bias,
        second_gain,
        second_shift,
        embed_table,
    ) = weights
    embedded = jnp.dot(onehot, embed_table, preferred_element_type=jnp.float32)
    start = jnp.where(chosen, embedded, tokens.astype(jnp.float32))
    start_low = start.astype(jnp.bfloat16)
    qkv_bias = jnp.concatenate([query_bias, jnp.zeros_like(query_bias), value_bias]).astype(
        jnp.float32
    )
    qkv_low = (
        jnp.dot(start_low, qkv_weight, preferred_element_type=jnp.float32) + qkv_bias
    ).astype(jnp.bfloat16)
    pages = qkv_low.reshape(-1, SEQ, 3, HEADS, HEAD)
    mixed, logsum = lax.map(attend, pages)
    attended = mixed.reshape(-1, D).astype(jnp.bfloat16)
    projected = jnp.dot(
        attended, proj_weight, preferred_element_type=jnp.float32
    ) + proj_bias.astype(jnp.float32)
    hidden_one = start + projected
    first = plain_norm_rows(hidden_one, first_gain.astype(jnp.float32), first_shift.astype(jnp.float32))
    first_low = first.astype(jnp.bfloat16)
    inner = jnp.dot(
        first_low, inner_weight, preferred_element_type=jnp.float32
    ) + inner_bias.astype(jnp.float32)
    active = jax.nn.gelu(inner, approximate=False).astype(jnp.bfloat16)
    outer = jnp.dot(active, outer_weight, preferred_element_type=jnp.float32) + outer_bias.astype(
        jnp.float32
    )
    hidden_two = first + outer
    return (start_low, qkv_low, logsum, attended, hidden_one, first_low, inner, active, hidden_two)


def local_plain(
    tokens,
    masked_rows,
    replace_ids,
    cotangent,
    qkv_weight,
    query_bias,
    value_bias,
    proj_weight,
    proj_bias,
    first_gain,
    first_shift,
    inner_weight,
    inner_bias,
    outer_weight,
    outer_bias,
    second_gain,
    second_shift,
    embed_table,
):
    weights = (
        lax.all_gather(qkv_weight, "fsdp", axis=1, tiled=True),
        lax.all_gather(query_bias, "fsdp", axis=0, tiled=True),
        lax.all_gather(value_bias, "fsdp", axis=0, tiled=True),
        lax.all_gather(proj_weight, "fsdp", axis=1, tiled=True),
        lax.all_gather(proj_bias, "fsdp", axis=0, tiled=True),
        lax.all_gather(first_gain, "fsdp", axis=0, tiled=True),
        lax.all_gather(first_shift, "fsdp", axis=0, tiled=True),
        lax.all_gather(inner_weight, "fsdp", axis=1, tiled=True),
        lax.all_gather(inner_bias, "fsdp", axis=0, tiled=True),
        lax.all_gather(outer_weight, "fsdp", axis=0, tiled=True),
        lax.all_gather(outer_bias, "fsdp", axis=0, tiled=True),
        lax.all_gather(second_gain, "fsdp", axis=0, tiled=True),
        lax.all_gather(second_shift, "fsdp", axis=0, tiled=True),
        lax.all_gather(embed_table, "fsdp", axis=0, tiled=True),
    )
    chosen = masked_rows[:, None] > 0
    onehot = (replace_ids[:, None] == jnp.arange(TABLE, dtype=jnp.int32)[None, :]).astype(
        jnp.bfloat16
    )
    saved = plain_forward(weights, tokens, chosen, onehot)
    layer_out = plain_norm_rows(
        saved[8], weights[11].astype(jnp.float32), weights[12].astype(jnp.float32)
    ).astype(jnp.bfloat16)
    back_weights = (
        lax.all_gather(qkv_weight, "fsdp", axis=1, tiled=True),
        lax.all_gather(query_bias, "fsdp", axis=0, tiled=True),
        lax.all_gather(value_bias, "fsdp", axis=0, tiled=True),
        lax.all_gather(proj_weight, "fsdp", axis=1, tiled=True),
        lax.all_gather(proj_bias, "fsdp", axis=0, tiled=True),
        lax.all_gather(first_gain, "fsdp", axis=0, tiled=True),
        lax.all_gather(first_shift, "fsdp", axis=0, tiled=True),
        lax.all_gather(inner_weight, "fsdp", axis=1, tiled=True),
        lax.all_gather(inner_bias, "fsdp", axis=0, tiled=True),
        lax.all_gather(outer_weight, "fsdp", axis=0, tiled=True),
        lax.all_gather(outer_bias, "fsdp", axis=0, tiled=True),
        lax.all_gather(second_gain, "fsdp", axis=0, tiled=True),
        lax.all_gather(second_shift, "fsdp", axis=0, tiled=True),
        lax.all_gather(embed_table, "fsdp", axis=0, tiled=True),
    )
    saved = plain_forward(back_weights, tokens, chosen, onehot)
    start_low, qkv_low, logsum, attended, hidden_one, first_low, inner, active, hidden_two = saved
    (
        full_qkv,
        full_query_bias,
        full_value_bias,
        full_proj,
        full_proj_bias,
        full_first_gain,
        full_first_shift,
        full_inner,
        full_inner_bias,
        full_outer,
        full_outer_bias,
        full_second_gain,
        full_second_shift,
        full_table,
    ) = back_weights
    grad_out = jnp.where(chosen, cotangent.astype(jnp.float32), 0.0)
    grad_two, grad_second_gain, grad_second_shift = plain_norm_back(
        hidden_two, full_second_gain, full_second_shift, grad_out
    )
    grad_outer_low = grad_two.astype(jnp.bfloat16)
    grad_outer_bias = jnp.sum(grad_outer_low, axis=0, dtype=jnp.float32)
    grad_outer_weight = jnp.dot(active.T, grad_outer_low, preferred_element_type=jnp.float32)
    grad_active = jnp.dot(grad_outer_low, full_outer.T, preferred_element_type=jnp.float32)
    _, gelu_pull = jax.vjp(partial(jax.nn.gelu, approximate=False), inner)
    grad_inner_low = gelu_pull(grad_active)[0].astype(jnp.bfloat16)
    grad_inner_bias = jnp.sum(grad_inner_low, axis=0, dtype=jnp.float32)
    grad_inner_weight = jnp.dot(first_low.T, grad_inner_low, preferred_element_type=jnp.float32)
    grad_first = grad_two + jnp.dot(
        grad_inner_low, full_inner.T, preferred_element_type=jnp.float32
    )
    grad_one, grad_first_gain, grad_first_shift = plain_norm_back(
        hidden_one, full_first_gain, full_first_shift, grad_first
    )
    grad_proj_low = grad_one.astype(jnp.bfloat16)
    grad_proj_bias = jnp.sum(grad_proj_low, axis=0, dtype=jnp.float32)
    grad_proj_weight = jnp.dot(attended.T, grad_proj_low, preferred_element_type=jnp.float32)
    grad_attended = jnp.dot(grad_proj_low, full_proj.T, preferred_element_type=jnp.float32).astype(
        jnp.bfloat16
    )
    grad_pages = lax.map(
        attend_back,
        (
            qkv_low.reshape(-1, SEQ, 3, HEADS, HEAD),
            logsum,
            grad_attended.reshape(-1, SEQ, HEADS, HEAD),
        ),
    )
    grad_qkv_low = grad_pages.reshape(-1, 3 * D).astype(jnp.bfloat16)
    grad_query_bias = jnp.sum(grad_qkv_low[:, :D], axis=0, dtype=jnp.float32)
    grad_value_bias = jnp.sum(grad_qkv_low[:, 2 * D :], axis=0, dtype=jnp.float32)
    grad_qkv_weight = jnp.dot(start_low.T, grad_qkv_low, preferred_element_type=jnp.float32)
    grad_start = grad_one + jnp.dot(grad_qkv_low, full_qkv.T, preferred_element_type=jnp.float32)
    token_grad = jnp.where(chosen, 0.0, grad_start)
    grad_embed_low = jnp.where(chosen, grad_start, 0.0).astype(jnp.bfloat16)
    grad_table = jnp.dot(onehot.T, grad_embed_low, preferred_element_type=jnp.float32)
    shards = (
        lax.psum_scatter(
            grad_qkv_weight.astype(jnp.bfloat16), "fsdp", scatter_dimension=1, tiled=True
        ).astype(jnp.float32),
        lax.psum_scatter(
            grad_query_bias.astype(jnp.bfloat16), "fsdp", scatter_dimension=0, tiled=True
        ).astype(jnp.float32),
        lax.psum_scatter(
            grad_value_bias.astype(jnp.bfloat16), "fsdp", scatter_dimension=0, tiled=True
        ).astype(jnp.float32),
        lax.psum_scatter(
            grad_proj_weight.astype(jnp.bfloat16), "fsdp", scatter_dimension=1, tiled=True
        ).astype(jnp.float32),
        lax.psum_scatter(
            grad_proj_bias.astype(jnp.bfloat16), "fsdp", scatter_dimension=0, tiled=True
        ).astype(jnp.float32),
        lax.psum_scatter(
            grad_first_gain.astype(jnp.bfloat16), "fsdp", scatter_dimension=0, tiled=True
        ).astype(jnp.float32),
        lax.psum_scatter(
            grad_first_shift.astype(jnp.bfloat16), "fsdp", scatter_dimension=0, tiled=True
        ).astype(jnp.float32),
        lax.psum_scatter(
            grad_inner_weight.astype(jnp.bfloat16), "fsdp", scatter_dimension=1, tiled=True
        ).astype(jnp.float32),
        lax.psum_scatter(
            grad_inner_bias.astype(jnp.bfloat16), "fsdp", scatter_dimension=0, tiled=True
        ).astype(jnp.float32),
        lax.psum_scatter(
            grad_outer_weight.astype(jnp.bfloat16), "fsdp", scatter_dimension=0, tiled=True
        ).astype(jnp.float32),
        lax.psum_scatter(
            grad_outer_bias.astype(jnp.bfloat16), "fsdp", scatter_dimension=0, tiled=True
        ).astype(jnp.float32),
        lax.psum_scatter(
            grad_second_gain.astype(jnp.bfloat16), "fsdp", scatter_dimension=0, tiled=True
        ).astype(jnp.float32),
        lax.psum_scatter(
            grad_second_shift.astype(jnp.bfloat16), "fsdp", scatter_dimension=0, tiled=True
        ).astype(jnp.float32),
        lax.psum_scatter(
            grad_table.astype(jnp.bfloat16), "fsdp", scatter_dimension=0, tiled=True
        ).astype(jnp.float32),
    )
    summed = (
        lax.psum(shards[0].astype(jnp.bfloat16), "dp").astype(jnp.float32),
        lax.psum(shards[1].astype(jnp.bfloat16), "dp").astype(jnp.float32),
        lax.psum(shards[2].astype(jnp.bfloat16), "dp").astype(jnp.float32),
        lax.psum(shards[3].astype(jnp.bfloat16), "dp").astype(jnp.float32),
        lax.psum(shards[4].astype(jnp.bfloat16), "dp").astype(jnp.float32),
        lax.psum(shards[5].astype(jnp.bfloat16), "dp").astype(jnp.float32),
        lax.psum(shards[6].astype(jnp.bfloat16), "dp").astype(jnp.float32),
        lax.psum(shards[7].astype(jnp.bfloat16), "dp").astype(jnp.float32),
        lax.psum(shards[8].astype(jnp.bfloat16), "dp").astype(jnp.float32),
        lax.psum(shards[9].astype(jnp.bfloat16), "dp").astype(jnp.float32),
        lax.psum(shards[10].astype(jnp.bfloat16), "dp").astype(jnp.float32),
        lax.psum(shards[11].astype(jnp.bfloat16), "dp").astype(jnp.float32),
        lax.psum(shards[12].astype(jnp.bfloat16), "dp").astype(jnp.float32),
        lax.psum(shards[13].astype(jnp.bfloat16), "dp").astype(jnp.float32),
    )
    return (
        layer_out,
        token_grad,
        summed[0],
        summed[1],
        summed[2],
        summed[3],
        summed[4],
        summed[5],
        summed[6],
        summed[7],
        summed[8],
        summed[9],
        summed[10],
        summed[11],
        summed[12],
        summed[13],
    )


def solution(mesh):
    direct = mesh.shape["dp"] == 8 and mesh.shape["fsdp"] == 4
    return jax.shard_map(
        local_direct if direct else local_plain,
        mesh=mesh,
        in_specs=(
            P(("dp", "fsdp"), None),
            P(("dp", "fsdp")),
            P(("dp", "fsdp")),
            P(("dp", "fsdp"), None),
            P(None, "fsdp"),
            P("fsdp"),
            P("fsdp"),
            P(None, "fsdp"),
            P("fsdp"),
            P("fsdp"),
            P("fsdp"),
            P(None, "fsdp"),
            P("fsdp"),
            P("fsdp", None),
            P("fsdp"),
            P("fsdp"),
            P("fsdp"),
            P("fsdp", None),
        ),
        out_specs=(
            P(("dp", "fsdp"), None),
            P(("dp", "fsdp"), None),
            P(None, "fsdp"),
            P("fsdp"),
            P("fsdp"),
            P(None, "fsdp"),
            P("fsdp"),
            P("fsdp"),
            P("fsdp"),
            P(None, "fsdp"),
            P("fsdp"),
            P("fsdp", None),
            P("fsdp"),
            P("fsdp"),
            P("fsdp"),
            P("fsdp", None),
        ),
        check_vma=False,
    )
```

```python
import functools
from functools import partial

import jax
import jax.numpy as jnp
from jax import lax
from jax.experimental import pallas as pl
from jax.experimental.pallas import tpu as pltpu
from jax.sharding import PartitionSpec as P


SEQ, HEAD, HEADS, D, TABLE = 512, 64, 12, 768, 768
EPS = 1e-5
LOG2E = 1.4426950408889634
F32, BF16 = jnp.float32, jnp.bfloat16
MESH = pl.DeviceIdType.MESH

PART = 192
TAB, QKV, PROJ, INNER, OUTER, ITEMS = 0, 1, 4, 5, 9, 13
V_QUERY, V_VALUE, V_PROJ, V_GAIN1, V_SHIFT1, V_OUTER, V_GAIN2, V_SHIFT2 = range(4, 12)

def mm(a, b):
    return lax.dot_general(a, b, (((1,), (0,)), ((), ())), preferred_element_type=F32)

def mm_nt(a, b):
    return lax.dot_general(a, b, (((1,), (1,)), ((), ())), preferred_element_type=F32)

def upper_tail(size):
    t = pl.reciprocal(1.0 + (0.3275911 * 0.7071067811865476) * size, approx=True)
    bell = jnp.exp2(size * size * (-0.5 * LOG2E))
    poly = t * (0.127414796 + t * (-0.142248368 + t * (0.7107068705 + t * (-0.7265760135 + t * 0.5307027145))))
    return poly * bell, bell

def norm_parts(hidden):
    center = jnp.mean(hidden, axis=-1, keepdims=True)
    offset = hidden - center
    spread = jnp.mean(offset * offset, axis=-1, keepdims=True)
    inv = lax.rsqrt(spread + EPS)
    return offset * inv, inv

def row_of(vec_ref, k):
    return vec_ref[k, 0:1, :]

def place_vectors(fs, smalls, parts):
    for s in range(4):
        @pl.when(fs == s)
        def _():
            inner_bias = smalls[0][...].reshape(1, D)
            rows = [inner_bias[:, PART * j:PART * j + PART] for j in range(4)] + [v[...].reshape(1, PART) for v in smalls[1:]]
            rows.append(jnp.zeros((4, PART), BF16))
            mine = jnp.concatenate(rows, axis=0)
            sides = [jnp.zeros((16, PART * s), BF16)] * (s > 0) + [mine] + [jnp.zeros((16, D - PART * s - PART), BF16)] * (s < 3)
            parts[s] = jnp.concatenate(sides, axis=1)

def sum_vectors(parts_ref, vec_ref):
    total = parts_ref[0].astype(F32)
    for s in range(1, parts_ref.shape[0]):
        total = total + parts_ref[s].astype(F32)
    for k in range(12):
        vec_ref[k] = jnp.broadcast_to(total[k:k + 1, :], (8, D))

def item(ref, m):
    return ref[pl.ds(m * D if isinstance(m, int) else pl.multiple_of(m * D, D), D), :]

def embed_rows(idf, tokens, tab, start):
    lanes = lax.broadcasted_iota(jnp.int32, (128, 128), 1).astype(F32)
    def step(i, _):
        ids = jnp.broadcast_to(idf[pl.ds(i, 1), :], (128, 128)).T
        hot = jnp.concatenate([(ids == lanes + 128.0 * j).astype(F32).astype(BF16) for j in range(TABLE // 128)], axis=1)
        rows = pl.ds(pl.multiple_of(i * 128, 128), 128)
        emb = mm(hot, item(tab, TAB))
        kept = jnp.concatenate([ids] * (D // 128), axis=1) < 0.0
        start[rows, :] = jnp.where(kept, tokens[rows, :].astype(F32), emb).astype(BF16)
        return 0
    lax.fori_loop(0, idf.shape[0], step, 0)

def make_colbias(vec, colb):
    for part, k in ((0, V_QUERY), (1, None), (2, V_VALUE)):
        for j in range(D // 128):
            tile = jnp.zeros((128, 128), F32) if k is None else jnp.broadcast_to(vec[k, 0:1, 128 * j:128 * j + 128], (128, 128)).T
            colb[part * D + 128 * j:part * D + 128 * j + 128, :] = tile

def qkv_item(j, all_w, start, colb, qkvt):
    @pl.loop(0, start.shape[0] // 256)
    def _(i):
        cols = pl.ds(pl.multiple_of(i * 256, 256), 256)
        acc = mm_nt(item(all_w, QKV + j), start[cols, :])
        for s in range(4):
            at = 3 * PART * s + PART * j
            bias = jnp.concatenate([colb[at:at + PART, :]] * 2, axis=1)
            qkvt[at:at + PART, cols] = (acc[PART * s:PART * s + PART] + bias).astype(BF16)

def attend_pair(page, pair, qkvt, att):
    cols = pl.ds(pl.multiple_of(page * SEQ, SEQ), SEQ)
    ones = jnp.ones((16, SEQ), BF16)
    outs = []
    for sub in range(2):
        head = pair * 2 + sub
        at = lambda part: pl.ds(pl.multiple_of(part * D + head * HEAD, HEAD), HEAD)
        qt = qkvt[at(0), cols]
        kn = qkvt[at(1), cols].T
        vt = jnp.concatenate([qkvt[at(2), cols], ones], axis=0)
        halves = []
        for c in range(2):
            s = mm(kn, qt[:, 256 * c:256 * c + 256])
            top = jnp.max(s, axis=0, keepdims=True)
            e = jnp.exp2((s - top) * (LOG2E * HEAD ** -0.5)).astype(BF16)
            o = mm(vt, e)
            halves.append(o[:HEAD] / o[HEAD:HEAD + 1])
        outs.append(jnp.concatenate(halves, axis=1))
    both = jnp.concatenate(outs, axis=0)
    att[cols, pl.ds(pl.multiple_of(pair * 128, 128), 128)] = both.T.astype(BF16)

def proj_norm(i, size, att, all_w, start, vec, acc, low):
    rows = pl.ds(pl.multiple_of(i * size, size), size)
    h = start[rows, :].astype(F32) + (mm_nt(att[rows, :], item(all_w, PROJ)) + row_of(vec, V_PROJ))
    xhat, _ = norm_parts(h)
    first = xhat * row_of(vec, V_GAIN1) + row_of(vec, V_SHIFT1)
    low[rows, :] = first.astype(BF16)
    acc[rows, :] = first + row_of(vec, V_OUTER)

def ff_part(j, i, size, low, all_w, vec, acc):
    rows = pl.ds(pl.multiple_of(i * size, size), size)
    x = mm_nt(low[rows, :], item(all_w, INNER + j)) + row_of(vec, j)
    a = jnp.abs(x)
    q, _ = upper_tail(a)
    active = (jnp.maximum(x, 0.0) - a * q).astype(BF16)
    acc[rows, :] += mm(active, item(all_w, OUTER + j))

def out_norm(i, size, acc, vec, out):
    rows = pl.ds(pl.multiple_of(i * size, size), size)
    xhat, _ = norm_parts(acc[rows, :])
    out[rows, :] = (xhat * row_of(vec, V_GAIN2) + row_of(vec, V_SHIFT2)).astype(BF16)

def fwd_kernel(tokens, masked, ids, tab_own, qkv_own, proj_own, inner_own, outer_own, *rest):
    smalls, rest = rest[:9], rest[9:]
    (out, start, att, qkvt, w_out, vec, idf,
     all_w, parts, colb, acc, low, send_sem, recv_sem, vsend, vrecv, own_sem, out_sem) = rest
    T = tokens.shape[0]
    pages = T // SEQ
    dp, fs = lax.axis_index("dp"), lax.axis_index("fsdp")
    y, c = fs // 2, fs % 2
    x, z = dp % 2, (dp // 2) % 2
    to_c, to_y = (dp, 2 * y + 1 - c), (dp, 2 * (1 - y) + c)
    to_x, to_z = (dp + 1 - 2 * x, fs), (dp + 2 - 4 * z, fs)
    across = 2 * (1 - y) + c
    part = PART // 4
    spot = [part * (x + 2 * z), part * (1 - x + 2 * z), part * (x + 2 * (1 - z)), part * (1 - x + 2 * (1 - z))]

    def rows_of(m, s, at=0, size=PART):
        return pl.ds(pl.multiple_of(m * D + PART * s + at, 16), size)

    own_copies = []
    for src, m, count in ((tab_own, TAB, 1), (qkv_own, QKV, 3), (proj_own, PROJ, 1), (outer_own, OUTER, 4)):
        for j in range(count):
            own_copies.append(pltpu.make_async_copy(src.at[pl.ds(PART * j, PART)], all_w.at[rows_of(m + j, fs)], own_sem.at[len(own_copies)]))
    for k in own_copies:
        k.start()
    idf[...] = jnp.where(masked[...] > 0, ids[...], -1).astype(F32)
    place_vectors(fs, smalls, parts)

    barrier = pltpu.get_barrier_semaphore()
    for to in (to_c, to_y, to_x, to_z):
        pl.semaphore_signal(barrier, inc=1, device_id=to, device_id_type=MESH)
    pl.semaphore_wait(barrier, 4)

    first, second = 2 * part // 3, part // 3
    kinds = [
        (0, PART, fs, to_c), (spot[0], part, fs, to_y),
        (spot[0], part, across, to_x), (spot[0], part, across, to_z), (spot[0], part, across, to_c),
        (spot[1], part, across, to_c), (spot[1] + first, second, across, to_z),
        (spot[2], part, across, to_c), (spot[2], first, across, to_x),
        (spot[3], first, across, to_c), (spot[3] + first, second, across, to_c),
    ]

    def copy(m, k):
        at, size, owner, to = kinds[k]
        rows = rows_of(m, owner, at, size)
        return pltpu.make_async_remote_copy(src_ref=all_w.at[rows], dst_ref=all_w.at[rows], send_sem=send_sem.at[m, k], recv_sem=recv_sem.at[m, k],
                                            device_id=to, device_id_type=MESH)

    def begin(m):
        if m == TAB:
            own_copies[0].wait()
        if m == QKV:
            for k in range(1, 5):
                own_copies[k].wait()
        if m == INNER:
            flipped = inner_own[...].T
            for j in range(4):
                all_w[rows_of(INNER + j, fs), :] = flipped[PART * j:PART * j + PART]
        if m >= OUTER:
            own_copies[5 + m - OUTER].wait()
        copy(m, 1).start()
        copy(m, 0).start()

    def from_y(m):
        copy(m, 1).wait_recv()
        for k in (2, 3, 4):
            copy(m, k).start()

    def from_sides(m):
        copy(m, 2).wait_recv()
        copy(m, 6).start()
        copy(m, 5).start()
        copy(m, 3).wait_recv()
        copy(m, 8).start()
        copy(m, 7).start()

    def from_corner(m):
        copy(m, 8).wait_recv()
        copy(m, 9).start()
        copy(m, 6).wait_recv()
        copy(m, 10).start()

    leave = lambda m: pltpu.make_async_copy(all_w.at[pl.ds(m * D, D)], w_out.at[pl.ds(m * D, D)], out_sem.at[m])

    def complete(m):
        for k in (0, 4, 5, 7, 9, 10):
            copy(m, k).wait_recv()
        if m != TAB:
            leave(m).start()

    def vec_copy(k):
        rows = parts.at[fs] if k < 2 else parts.at[across]
        return pltpu.make_async_remote_copy(src_ref=rows, dst_ref=rows, send_sem=vsend.at[k], recv_sem=vrecv.at[k], device_id=(to_y, to_c, to_c)[k], device_id_type=MESH)

    begin(0)
    vec_copy(0).start()
    vec_copy(1).start()
    begin(1)
    begin(2)
    begin(3)
    from_y(0)
    vec_copy(0).wait_recv()
    vec_copy(2).start()
    begin(4)
    from_y(1)
    from_sides(0)
    from_y(2)
    from_sides(1)
    from_corner(0)
    vec_copy(1).wait_recv()
    vec_copy(2).wait_recv()
    sum_vectors(parts, vec)
    make_colbias(vec, colb)
    complete(0)
    embed_rows(idf, tokens, all_w, start)
    begin(5)
    for j in range(3):
        from_y(3 + j)
        from_sides(2 + j)
        from_corner(1 + j)
        complete(1 + j)
        begin(6 + j)
        qkv_item(j, all_w, start, colb, qkvt)

    @pl.loop(0, pages * 6)
    def _(it):
        for m in range(PROJ, ITEMS):
            for stage, first, when in ((complete, PROJ, m - 1), (from_corner, PROJ, m - 2), (from_sides, PROJ + 1, m - 4), (from_y, PROJ + 2, m - 6), (begin, PROJ + 5, m - 9)):
                if m >= first:
                    @pl.when(it == when)
                    def _():
                        stage(m)
        attend_pair(it // 6, it % 6, qkvt, att)

    @pl.loop(0, T // 256)
    def _(i):
        proj_norm(i, 256, att, all_w, start, vec, acc, low)
    @pl.loop(0, 4 * (T // 512))
    def _(it):
        ff_part(it // (T // 512), it % (T // 512), 512, low, all_w, vec, acc)
    @pl.loop(0, T // 256)
    def _(i):
        out_norm(i, 256, acc, vec, out)
    for m in range(ITEMS):
        for k in range(len(kinds)):
            copy(m, k).wait_send()
        if m != TAB:
            leave(m).wait()
    for k in range(3):
        vec_copy(k).wait_send()

def forward_call(tokens, masked, ids, tab, qkv, proj, inner, outer, smalls):
    T = tokens.shape[0]
    vm = pl.BlockSpec(memory_space=pltpu.VMEM)
    hb = pl.BlockSpec(memory_space=pl.ANY)
    shp = jax.ShapeDtypeStruct
    dma = pltpu.SemaphoreType.DMA
    return pl.pallas_call(
        fwd_kernel,
        out_shape=[shp((T, D), BF16), shp((T, D), BF16), shp((T, D), BF16), shp((3 * D, T), BF16), shp((ITEMS * D, D), BF16), shp((12, 8, D), F32), shp((T // 128, 128), F32)],
        in_specs=[vm, vm, vm, hb, hb, hb, vm, hb] + [vm] * 9, out_specs=[vm] * 4 + [hb, vm, vm],
        scratch_shapes=[pltpu.VMEM((ITEMS * D, D), BF16), pltpu.VMEM((4, 16, D), BF16), pltpu.VMEM((3 * D, 128), F32), pltpu.VMEM((T, D), F32), pltpu.VMEM((T, D), BF16),
                        dma((ITEMS, 11)), dma((ITEMS, 11)), dma((3,)), dma((3,)), dma((9,)), dma((ITEMS,))],
        compiler_params=pltpu.CompilerParams(collective_id=0, has_side_effects=True, vmem_limit_bytes=60 * 2**20), name="forward",
    )(tokens, masked, ids, tab, qkv, proj, inner, outer, *smalls)


HALF = 128
VEC_ROWS = 64

def mm_tn(a, b):
    return mm(a.T, b)

def norm_back(xhat, inv, gain, g):
    gx = g * gain
    return inv * (gx - jnp.mean(gx, axis=-1, keepdims=True) - xhat * jnp.mean(gx * xhat, axis=-1, keepdims=True))

def put(ref, index, value, first):
    if first:
        ref[index] = value.astype(ref.dtype)
    else:
        ref[index] = (ref[index].astype(F32) + value).astype(ref.dtype)

def add(sums, k, values):
    sums[k] += jnp.sum(values.reshape(-1, 8, values.shape[-1]), axis=0)

def item_row(row):
    block = row // PART
    return ((block % 3) * 4 + block // 3) * PART + row % PART

def split(v):
    high = v.astype(BF16)
    return high, (v - high.astype(F32)).astype(BF16)

def bwd_kernel(idf, vec, out_h, start_h, att_h, cot_h, qkvt_h, w_h, grad_h, gvec, token_h, layer_out,
               start, att, cot, qkvt, w, grad, tok, active, slope, low, acc, xhat_one, g_first, qct, gact, gone, gqt, sums, pick, rank, stage, tacc, sem_in, sem_out):
    T = start.shape[0]
    pages = T // SEQ
    per = SEQ // 128
    base = PROJ
    span = lambda a, b: (w_h.at[pl.ds(a * D, (b - a) * D)], w.at[pl.ds((a - base) * D, (b - a) * D)])
    arrivals = {}
    for k, (name, src, dst) in enumerate((("start", start_h, start), ("att", att_h, att), ("proj",) + span(PROJ, INNER), ("inner",) + span(INNER, OUTER),
                                          ("outer",) + span(OUTER, ITEMS), ("cot", cot_h, cot), ("qkvt", qkvt_h, qkvt))):
        arrivals[name] = pltpu.make_async_copy(src, dst, sem_in.at[k])
        arrivals[name].start()
    weight = lambda m: item(w, m - base)
    pass_on = pltpu.make_async_copy(out_h, layer_out, sem_in.at[8])
    pass_on.start()

    r_i = lax.broadcasted_iota(jnp.int32, (SEQ, SEQ), 0)
    c_i = lax.broadcasted_iota(jnp.int32, (SEQ, SEQ), 1)
    upper = (r_i < c_i).astype(F32).astype(BF16)
    for p in range(pages):
        ids = jnp.concatenate([idf[per * p + k:per * p + k + 1, :] for k in range(per)], axis=1)
        ids8 = jnp.broadcast_to(ids, (8, SEQ))
        hit = (ids8 >= 0.0).astype(F32)
        before = mm(jnp.concatenate([hit, hit], axis=0).astype(BF16), upper)[:8]
        rank[p] = jnp.where(ids8 >= 0.0, before, -1e6)
    sums[...] = jnp.zeros_like(sums)
    row_j = lax.broadcasted_iota(jnp.int32, (HALF, SEQ), 0).astype(F32)

    def picked(ref):
        return jnp.concatenate([mm(pick[p], ref[p * SEQ:(p + 1) * SEQ, :]) for p in range(pages)], axis=0)

    def block(b, first):
        wait = (lambda n: arrivals[n].wait()) if first else (lambda n: None)
        offset = float(b * HALF) if first else (b * HALF).astype(F32)
        for p in range(pages):
            pick[p] = (jnp.broadcast_to(rank[p][0:1, :], (HALF, SEQ)) == row_j + offset).astype(F32).astype(BF16)
        wait("start"); wait("att"); wait("proj")
        att_c = picked(att).astype(BF16)
        h = picked(start) + (mm_nt(att_c, weight(PROJ)) + row_of(vec, V_PROJ))
        xhat, inv_one = norm_parts(h)
        xhat_one[...] = xhat
        f = xhat * row_of(vec, V_GAIN1) + row_of(vec, V_SHIFT1)
        low[...] = f.astype(BF16)
        acc[...] = f + row_of(vec, V_OUTER)
        wait("inner"); wait("outer")
        @pl.loop(0, 4)
        def _(j):
            x = mm_nt(low[...], weight(INNER + j)) + row_of(vec, j)
            a = jnp.abs(x)
            q, bell = upper_tail(a)
            active[j] = (jnp.maximum(x, 0.0) - a * q).astype(BF16)
            slope[j] = (jnp.where(x >= 0.0, 1.0 - q, q) + x * (bell * 0.3989422804014327)).astype(BF16)
            acc[...] += mm(active[j], weight(OUTER + j))
        xhat_two, inv_two = norm_parts(acc[...])
        wait("cot")
        g_out = picked(cot)
        add(sums, V_GAIN2, g_out * xhat_two)
        add(sums, V_SHIFT2, g_out)
        g_two = norm_back(xhat_two, inv_two, row_of(vec, V_GAIN2), g_out)
        g_outer = g_two.astype(BF16)
        add(sums, V_OUTER, g_outer.astype(F32))
        g_first[...] = g_two
        @pl.loop(0, 4)
        def _(j):
            put(grad, (pl.ds(pl.multiple_of((OUTER + j) * D, D), D),), mm_tn(active[j], g_outer), first)
            g_inner = (mm_nt(g_outer, weight(OUTER + j)) * slope[j].astype(F32)).astype(BF16)
            add(sums, j, g_inner.astype(F32))
            put(grad, (pl.ds(pl.multiple_of((INNER + j) * D, D), D),), mm_tn(g_inner, low[...]), first)
            g_first[...] += mm(g_inner, weight(INNER + j))
        g = g_first[...]
        xhat = xhat_one[...]
        add(sums, V_GAIN1, g * xhat)
        add(sums, V_SHIFT1, g)
        g_one = norm_back(xhat, inv_one, row_of(vec, V_GAIN1), g)
        high, rest = split(g_one)
        for p in range(pages):
            back = pick[p].T
            mine = slice(p * HALF, (p + 1) * HALF)
            put(gone, (slice(p * SEQ, (p + 1) * SEQ),), mm(back, high[mine]) + mm(back, rest[mine]), first)
        g_proj = high
        add(sums, V_PROJ, g_proj.astype(F32))
        put(grad, (pl.ds(PROJ * D, D),), mm_tn(g_proj, att_c), first)
        gact[...] = mm(g_proj, weight(PROJ)).astype(BF16).T
        wait("qkvt")
        for p in range(pages):
            qct[:, p * HALF:(p + 1) * HALF] = mm_nt(qkvt[0:D, p * SEQ:(p + 1) * SEQ], pick[p]).astype(BF16)
        @pl.loop(0, pages * 6)
        def _(it):
            page, pair = it // 6, it % 6
            cols = pl.ds(pl.multiple_of(page * SEQ, SEQ), SEQ)
            small = pl.ds(pl.multiple_of(page * HALF, HALF), HALF)
            for sub in range(2):
                head = pair * 2 + sub
                at = lambda part: pl.ds(pl.multiple_of(part * D + head * HEAD, HEAD), HEAD)
                to = lambda part: pl.ds(pl.multiple_of(item_row(part * D + head * HEAD), HEAD), HEAD)
                kt = qkvt[at(1), cols]
                vn = qkvt[at(2), cols].T
                qt = qct[at(0), small]
                ga = gact[at(0), small]
                s = mm(kt.T, qt)
                top = jnp.max(s, axis=0, keepdims=True)
                e = jnp.exp2((s - top) * (LOG2E * HEAD ** -0.5))
                p = e * (1.0 / jnp.sum(e, axis=0, keepdims=True))
                gp = mm(vn, ga)
                d = jnp.sum(p * gp, axis=0, keepdims=True)
                gs = (p * (gp - d) * HEAD ** -0.5).astype(BF16)
                put(gqt, (to(0), cols), mm(mm(kt, gs).astype(BF16), pick[page]), first)
                put(gqt, (to(1), cols), mm_nt(qt, gs), first)
                put(gqt, (to(2), cols), mm_nt(ga, p.astype(BF16)), first)

    most = functools.reduce(jnp.maximum, [jnp.sum((idf[per * p:per * p + per, :] >= 0.0).astype(F32)) for p in range(pages)])
    nb = (most.astype(jnp.int32) + HALF - 1) // HALF
    block(0, True)
    @pl.loop(1, nb)
    def _(b):
        block(b, False)

    qkv_w = pltpu.make_async_copy(w_h.at[pl.ds(QKV * D, 3 * D)], w.at[pl.ds((OUTER - base) * D, 3 * D)], sem_in.at[7])
    qkv_w.start()
    early = pltpu.make_async_copy(grad.at[pl.ds(PROJ * D, (ITEMS - PROJ) * D)], grad_h.at[pl.ds(PROJ * D, (ITEMS - PROJ) * D)], sem_out.at[0])
    early.start()
    @pl.loop(0, 3)
    def _(j):
        rows = pl.ds(pl.multiple_of(j * D, D), D)
        grad[pl.ds(pl.multiple_of((QKV + j) * D, D), D), :] = mm(gqt[rows, :], start[...]).astype(BF16)
    middle = pltpu.make_async_copy(grad.at[pl.ds(QKV * D, 3 * D)], grad_h.at[pl.ds(QKV * D, 3 * D)], sem_out.at[1])
    middle.start()
    stage[...] = jnp.zeros_like(stage)
    for k in range(12):
        stage[k:k + 1, :] = jnp.sum(sums[k], axis=0, keepdims=True)
    ones = jnp.ones((16, T), BF16)
    for k, part in ((12, 0), (16, 2)):
        for i in range(4):
            at = item_row(part * D + PART * i)
            stage[k + i:k + i + 1, 0:PART] = mm_nt(ones, gqt[at:at + PART, :])[0:1]
    gvec[...] = stage[...].astype(BF16)
    qkv_w.wait()
    tacc[...] = jnp.zeros_like(tacc)
    r_i = lax.broadcasted_iota(jnp.int32, (TABLE, 256), 0).astype(F32)
    def leave(i, slot):
        rows = pl.ds(i * 256 if isinstance(i, int) else pl.multiple_of(i * 256, 256), 256)
        return pltpu.make_async_copy(tok.at[slot], token_h.at[rows], sem_out.at[2 + slot])
    @pl.loop(0, T // 256)
    def _(i):
        rows = pl.ds(pl.multiple_of(i * 256, 256), 256)
        gt = gqt[:, rows].T
        g = gone[rows, :]
        for j in range(3):
            g = g + mm(gt[:, D * j:D * j + D], item(w, OUTER - base + j))
        slot = i % 2
        @pl.when(i >= 2)
        def _():
            leave(i - 2, slot).wait()
        lows = []
        for k in range(2):
            ids = jnp.broadcast_to(idf[pl.ds(2 * i + k, 1), :], (128, 128)).T
            kept = jnp.concatenate([ids] * (D // 128), axis=1) < 0.0
            here = g[128 * k:128 * k + 128]
            tok[slot, 128 * k:128 * k + 128, :] = jnp.where(kept, here, 0.0)
            lows.append(jnp.where(kept, 0.0, here).astype(BF16))
        leave(i, slot).start()
        ids = jnp.concatenate([idf[pl.ds(2 * i, 1), :], idf[pl.ds(2 * i + 1, 1), :]], axis=1)
        hot = (jnp.broadcast_to(ids, (TABLE, 256)) == r_i).astype(F32).astype(BF16)
        tacc[...] += mm(hot, jnp.concatenate(lows, axis=0))
    grad[0:D, :] = tacc[...].astype(BF16)
    late = pltpu.make_async_copy(grad.at[pl.ds(0, D)], grad_h.at[pl.ds(0, D)], sem_out.at[4])
    late.start()
    early.wait()
    middle.wait()
    for i in range(T // 256 - 2, T // 256):
        leave(i, i % 2).wait()
    late.wait()
    pass_on.wait()

def backward_call(idf, vec, out, start, att, cot, qkvt, w):
    T = start.shape[0]
    pages = T // SEQ
    W = pages * HALF
    vm = pl.BlockSpec(memory_space=pltpu.VMEM)
    hb = pl.BlockSpec(memory_space=pl.ANY)
    f32 = lambda *s: pltpu.VMEM(s, F32)
    low = lambda *s: pltpu.VMEM(s, BF16)
    return pl.pallas_call(
        bwd_kernel,
        out_shape=[jax.ShapeDtypeStruct((ITEMS * D, D), BF16), jax.ShapeDtypeStruct((VEC_ROWS, D), BF16), jax.ShapeDtypeStruct((T, D), F32), jax.ShapeDtypeStruct((T, D), BF16)],
        in_specs=[vm, vm] + [hb] * 6, out_specs=[hb, vm, hb, hb],
        scratch_shapes=[low(T, D), low(T, D), low(T, D), low(3 * D, T), low((ITEMS - PROJ) * D, D), low(ITEMS * D, D), f32(2, 256, D),
                        low(4, W, D), low(4, W, D), low(W, D), f32(W, D), f32(W, D), f32(W, D), low(D, W), low(D, W), f32(T, D), low(3 * D, T),
                        f32(12, 8, D), low(pages, HALF, SEQ), f32(pages, 8, SEQ), f32(VEC_ROWS, D), f32(TABLE, D),
                        pltpu.SemaphoreType.DMA((9,)), pltpu.SemaphoreType.DMA((5,))],
        compiler_params=pltpu.CompilerParams(vmem_limit_bytes=62 * 2**20), name="backward",
    )(idf, vec, out, start, att, cot, qkvt, w)


CHUNK = 64
LAGS = (0, 2, 4, 6, 8, 10, 12)

def reduce_kernel(grad, gvec, fin_h, own, rc, sy, ry, kx, sx, rx, kz, sz, rz, se, re, fin, send_sem, recv_sem, own_sem, out_sem, vsend, vrecv):
    dp, fs = lax.axis_index("dp"), lax.axis_index("fsdp")
    y, c = fs // 2, fs % 2
    x, za, zb = dp % 2, (dp // 2) % 2, dp // 4
    to_c = (dp, 2 * y + 1 - c)
    to_y = (dp, 2 * (1 - y) + c)
    to_x = (dp + 1 - 2 * x, fs)
    to_a = (dp + 2 - 4 * za, fs)
    to_b = (dp + 4 - 8 * zb, fs)
    barrier = pltpu.get_barrier_semaphore()
    for to in (to_c, to_y, to_x, to_a, to_b):
        pl.semaphore_signal(barrier, inc=1, device_id=to, device_id_type=MESH)
    pl.semaphore_wait(barrier, 5)
    n = own.shape[1] // CHUNK
    H, Q = CHUNK // 2, CHUNK // 4
    rows = lambda k: pl.ds(pl.multiple_of(k * CHUNK, CHUNK), CHUNK)
    half = lambda k, s: pl.ds(pl.multiple_of(k * CHUNK + s * H, H), H)
    quarter = lambda k, s, t: pl.ds(pl.multiple_of(k * CHUNK + s * H + t * Q, Q), Q)
    hrows = lambda k: pl.ds(pl.multiple_of(k * H, H), H)
    qrows = lambda k: pl.ds(pl.multiple_of(k * Q, Q), Q)
    f = lambda v: v.astype(F32)

    def remote(stage, k, src, dst, to):
        return pltpu.make_async_remote_copy(src_ref=src, dst_ref=dst, send_sem=send_sem.at[stage, k], recv_sem=recv_sem.at[stage, k], device_id=to, device_id_type=MESH)
    copies = [
        None,
        lambda k: remote(1, k, sy.at[rows(k)], ry.at[rows(k)], to_y),
        lambda k: remote(2, k, sx.at[hrows(k)], rx.at[hrows(k)], to_x),
        lambda k: remote(3, k, sz.at[qrows(k)], rz.at[qrows(k)], to_a),
        lambda k: remote(4, k, se.at[qrows(k)], re.at[qrows(k)], to_b),
        lambda k: remote(5, k, fin.at[quarter(k, x, za)], fin.at[quarter(k, x, za)], to_a),
        lambda k: remote(6, k, fin.at[half(k, x)], fin.at[half(k, x)], to_x),
    ]
    per = PART // CHUNK
    chunk_of = lambda k, side: grad.at[ITEMS - 1 - k // per, :, side, pl.ds(pl.multiple_of((k % per) * CHUNK, CHUNK), CHUNK), :]
    copies[0] = lambda k: remote(0, k, chunk_of(k, 1 - c), rc.at[:, rows(k), :], to_c)
    local = lambda k: pltpu.make_async_copy(chunk_of(k, c), own.at[:, rows(k), :], own_sem.at[k])
    last = n - 1
    both = lambda ref: [(ref.at[s, pl.ds(last * CHUNK, CHUNK)], s) for s in range(2)]
    vec_local = [pltpu.make_async_copy(gvec, dst, own_sem.at[last + s]) for dst, s in both(own)]
    vec_remote = [pltpu.make_async_remote_copy(src_ref=gvec, dst_ref=dst, send_sem=vsend.at[s], recv_sem=vrecv.at[s], device_id=to_c, device_id_type=MESH) for dst, s in both(rc)]
    leave = lambda k: pltpu.make_async_copy(fin.at[rows(k)], fin_h.at[rows(k)], out_sem.at[k])

    for copy in vec_local + vec_remote:
        copy.start()
    @pl.loop(0, last)
    def _(k):
        copies[0](k).start()
        local(k).start()

    def on_y(k):
        @pl.when(k < last)
        def _():
            copies[0](k).wait_recv()
            local(k).wait()
        @pl.when(k == last)
        def _():
            for copy in vec_local:
                copy.wait()
            for copy in vec_remote:
                copy.wait_recv()
        sy[rows(k), :] = (f(own[1 - y, rows(k), :]) + f(rc[1 - y, rows(k), :])).astype(BF16)
        copies[1](k).start()

    def on_x(k):
        copies[1](k).wait_recv()
        part = lambda s: f(own[y, half(k, s), :]) + f(rc[y, half(k, s), :]) + f(ry[half(k, s), :])
        sx[hrows(k), :] = part(1 - x).astype(BF16)
        copies[2](k).start()
        kx[hrows(k), :] = part(x)

    def on_a(k):
        copies[2](k).wait_recv()
        part = lambda t: kx[pl.ds(pl.multiple_of(k * H + t * Q, Q), Q), :] + f(rx[pl.ds(pl.multiple_of(k * H + t * Q, Q), Q), :])
        sz[qrows(k), :] = part(1 - za).astype(BF16)
        copies[3](k).start()
        kz[qrows(k), :] = part(za)

    def on_b(k):
        copies[3](k).wait_recv()
        se[qrows(k), :] = (kz[qrows(k), :] + f(rz[qrows(k), :])).astype(BF16)
        copies[4](k).start()

    def back_a(k):
        copies[4](k).wait_recv()
        fin[quarter(k, x, za), :] = (f(se[qrows(k), :]) + f(re[qrows(k), :])).astype(BF16)
        copies[5](k).start()

    def back_x(k):
        copies[5](k).wait_recv()
        copies[6](k).start()

    def done(k):
        copies[6](k).wait_recv()
        leave(k).start()

    @pl.loop(0, n + LAGS[-1])
    def _(t):
        for stage, lag in zip((on_y, on_x, on_a, on_b, back_a, back_x, done), LAGS):
            k = t - lag
            @pl.when((k >= 0) & (k < n))
            def _():
                stage(k)

    @pl.loop(0, n)
    def _(k):
        for copy in copies[1:]:
            copy(k).wait_send()
        @pl.when(k < last)
        def _():
            copies[0](k).wait_send()
        leave(k).wait()
    for copy in vec_remote:
        copy.wait_send()

def reduce_call(grad, gvec):
    R = ITEMS * PART + VEC_ROWS
    n = R // CHUNK
    hb = pl.BlockSpec(memory_space=pl.ANY)
    low = lambda *s: pltpu.VMEM(s + (D,), BF16)
    return pl.pallas_call(
        reduce_kernel,
        out_shape=jax.ShapeDtypeStruct((R, D), BF16),
        in_specs=[hb, pl.BlockSpec(memory_space=pltpu.VMEM)], out_specs=hb,
        scratch_shapes=[low(2, R), low(2, R), low(R), low(R), pltpu.VMEM((R // 2, D), F32), low(R // 2), low(R // 2),
                        pltpu.VMEM((R // 4, D), F32), low(R // 4), low(R // 4), low(R // 4), low(R // 4), low(R),
                        pltpu.SemaphoreType.DMA((7, n)), pltpu.SemaphoreType.DMA((7, n)), pltpu.SemaphoreType.DMA((n + 1,)), pltpu.SemaphoreType.DMA((n,)), pltpu.SemaphoreType.DMA((2,)), pltpu.SemaphoreType.DMA((2,))],
        compiler_params=pltpu.CompilerParams(collective_id=1, has_side_effects=True, vmem_limit_bytes=60 * 2**20), name="reduce",
    )(grad.reshape(ITEMS, 2, 2, PART, D), gvec)

def finish_kernel(fin_h, outer_h, inner_h, qkv_h, proj_h, table_h, *rest):
    inner_b, smalls, (fin, outer, inner, qkv, proj, table, sem_in, sem_out) = rest[0], rest[1:9], rest[9:]
    edges = [0] + [(ITEMS - m) * PART for m in (OUTER, INNER, PROJ, QKV, TAB)] + [ITEMS * PART + VEC_ROWS]
    spans = [pl.ds(a, b - a) for a, b in zip(edges, edges[1:])]
    loads = [pltpu.make_async_copy(fin_h.at[r], fin.at[r], sem_in.at[k]) for k, r in enumerate(spans)]
    for copy in loads:
        copy.start()
    stores = []
    def leave(src, dst):
        stores.append(pltpu.make_async_copy(src, dst, sem_out.at[len(stores)]))
        stores[-1].start()
    at = lambda m: fin[(ITEMS - 1 - m) * PART:(ITEMS - m) * PART].astype(F32)
    loads[0].wait()
    for j in range(4):
        outer[PART * j:PART * j + PART, :] = at(OUTER + j)
    leave(outer, outer_h)
    loads[1].wait()
    inner[...] = jnp.concatenate([at(INNER + j) for j in range(4)], axis=0).T
    leave(inner, inner_h)
    loads[2].wait()
    proj[...] = at(PROJ)
    leave(proj, proj_h)
    loads[3].wait()
    for j in range(3):
        qkv[PART * j:PART * j + PART, :] = at(QKV + j)
    leave(qkv, qkv_h)
    loads[4].wait()
    table[...] = at(TAB)
    leave(table, table_h)
    loads[5].wait()
    rows = fin[ITEMS * PART:ITEMS * PART + VEC_ROWS].astype(F32)
    me = lax.axis_index("fsdp")
    def mine(k):
        return sum(jnp.where(me == s, rows[k, PART * s:PART * s + PART], 0.0) for s in range(4))
    for j in range(4):
        inner_b[pl.ds(PART * j, PART)] = mine(j)
    for k, ref in enumerate(smalls):
        if k < 2:
            ref[...] = sum(jnp.where(me == s, rows[12 + 4 * k + s, 0:PART], 0.0) for s in range(4))
        else:
            ref[...] = mine(4 + k)
    for copy in stores:
        copy.wait()

def finish_call(fin):
    vm = pl.BlockSpec(memory_space=pltpu.VMEM)
    hb = pl.BlockSpec(memory_space=pl.ANY)
    shapes = [(D, D), (D, D), (3 * PART, D), (PART, D), (PART, D)]
    shp = lambda *s: jax.ShapeDtypeStruct(s, F32)
    out = pl.pallas_call(
        finish_kernel, out_shape=[shp(*s) for s in shapes] + [shp(D)] + [shp(PART)] * 8,
        in_specs=[hb], out_specs=[hb] * 5 + [vm] * 9,
        scratch_shapes=[pltpu.VMEM(fin.shape, BF16)] + [pltpu.VMEM(s, F32) for s in shapes] + [pltpu.SemaphoreType.DMA((6,)), pltpu.SemaphoreType.DMA((5,))],
        compiler_params=pltpu.CompilerParams(vmem_limit_bytes=40 * 2**20), name="finish")(fin)
    outer, inner, qkv, proj, table, inner_b = out[:6]
    return outer, inner, qkv.T, proj.T, table, inner_b, out[6:]

def local_direct(tokens, masked_rows, replace_ids, cotangent, qkv_weight, query_bias, value_bias, proj_weight, proj_bias, first_gain, first_shift,
                 inner_weight, inner_bias, outer_weight, outer_bias, second_gain, second_shift, embed_table):
    smalls = (inner_bias, query_bias, value_bias, proj_bias, first_gain, first_shift, outer_bias, second_gain, second_shift)
    out, start, att, qkvt, w, vec, idf = forward_call(tokens, masked_rows.reshape(-1, 128), replace_ids.reshape(-1, 128), embed_table, qkv_weight.T, proj_weight.T,
                                                      inner_weight, outer_weight, smalls)
    grad, gvec, token_grad, layer_out = backward_call(idf, vec, out, start, att, cotangent, qkvt, w)
    outer, inner, qkv, proj, table, inner_b, smalls = finish_call(reduce_call(grad, gvec))
    q, v, pb, fg, fs, ob, sg, ss = smalls
    return (layer_out, token_grad, qkv, q, v, proj, pb, fg, fs, inner, inner_b, outer, ob, sg, ss, table)


def plain_norm_rows(hidden, gain, shift):
    center = jnp.mean(hidden, axis=-1, keepdims=True)
    offset = hidden - center
    spread = jnp.mean(offset * offset, axis=-1, keepdims=True)
    return offset * lax.rsqrt(spread + EPS) * gain + shift


def plain_norm_back(hidden, gain, shift, incoming):
    _, pull = jax.vjp(plain_norm_rows, hidden, gain.astype(jnp.float32), shift.astype(jnp.float32))
    return pull(incoming)


def attend(page_qkv):
    queries = page_qkv[:, 0]
    keys = page_qkv[:, 1]
    values = page_qkv[:, 2]
    scores = jnp.einsum(
        "qhd,khd->hqk", queries, keys, preferred_element_type=jnp.float32
    ) * HEAD ** (-0.5)
    largest = jnp.max(scores, axis=-1, keepdims=True)
    raised = jnp.exp(scores - largest)
    expsum = jnp.sum(raised, axis=-1, keepdims=True)
    probs = (raised / expsum).astype(jnp.bfloat16)
    mixed = jnp.einsum("hqk,khd->qhd", probs, values, preferred_element_type=jnp.float32)
    return (mixed.reshape(page_qkv.shape[0], D), (largest + jnp.log(expsum))[..., 0])


def attend_back(inputs_all):
    page_qkv, logsum, page_grad = inputs_all
    queries = page_qkv[:, 0]
    keys = page_qkv[:, 1]
    values = page_qkv[:, 2]
    scale = HEAD ** (-0.5)
    scores = jnp.einsum("qhd,khd->hqk", queries, keys, preferred_element_type=jnp.float32) * scale
    probs = jnp.exp(scores - logsum[..., None])
    probs_low = probs.astype(jnp.bfloat16)
    grad_prob = jnp.einsum("qhd,khd->hqk", page_grad, values, preferred_element_type=jnp.float32)
    grad_prob = lax.optimization_barrier(grad_prob.astype(jnp.bfloat16)).astype(jnp.float32)
    center = jnp.sum(probs * grad_prob, axis=-1, keepdims=True)
    grad_raw = (scale * probs * (grad_prob - center)).astype(jnp.bfloat16)
    grad_query = jnp.einsum("hqk,khd->qhd", grad_raw, keys, preferred_element_type=jnp.float32)
    grad_key = jnp.einsum("hqk,qhd->khd", grad_raw, queries, preferred_element_type=jnp.float32)
    grad_value = jnp.einsum(
        "hqk,qhd->khd", probs_low, page_grad, preferred_element_type=jnp.float32
    )
    stacked = jnp.stack([grad_query, grad_key, grad_value], axis=1)
    return stacked.reshape(page_qkv.shape[0], 3 * D)


def plain_forward(weights, tokens, chosen, onehot):
    (
        qkv_weight,
        query_bias,
        value_bias,
        proj_weight,
        proj_bias,
        first_gain,
        first_shift,
        inner_weight,
        inner_bias,
        outer_weight,
        outer_bias,
        second_gain,
        second_shift,
        embed_table,
    ) = weights
    embedded = jnp.dot(onehot, embed_table, preferred_element_type=jnp.float32)
    start = jnp.where(chosen, embedded, tokens.astype(jnp.float32))
    start_low = start.astype(jnp.bfloat16)
    qkv_bias = jnp.concatenate([query_bias, jnp.zeros_like(query_bias), value_bias]).astype(
        jnp.float32
    )
    qkv_low = (
        jnp.dot(start_low, qkv_weight, preferred_element_type=jnp.float32) + qkv_bias
    ).astype(jnp.bfloat16)
    pages = qkv_low.reshape(-1, SEQ, 3, HEADS, HEAD)
    mixed, logsum = lax.map(attend, pages)
    attended = mixed.reshape(-1, D).astype(jnp.bfloat16)
    projected = jnp.dot(
        attended, proj_weight, preferred_element_type=jnp.float32
    ) + proj_bias.astype(jnp.float32)
    hidden_one = start + projected
    first = plain_norm_rows(hidden_one, first_gain.astype(jnp.float32), first_shift.astype(jnp.float32))
    first_low = first.astype(jnp.bfloat16)
    inner = jnp.dot(
        first_low, inner_weight, preferred_element_type=jnp.float32
    ) + inner_bias.astype(jnp.float32)
    active = jax.nn.gelu(inner, approximate=False).astype(jnp.bfloat16)
    outer = jnp.dot(active, outer_weight, preferred_element_type=jnp.float32) + outer_bias.astype(
        jnp.float32
    )
    hidden_two = first + outer
    return (start_low, qkv_low, logsum, attended, hidden_one, first_low, inner, active, hidden_two)


def local_plain(
    tokens,
    masked_rows,
    replace_ids,
    cotangent,
    qkv_weight,
    query_bias,
    value_bias,
    proj_weight,
    proj_bias,
    first_gain,
    first_shift,
    inner_weight,
    inner_bias,
    outer_weight,
    outer_bias,
    second_gain,
    second_shift,
    embed_table,
):
    weights = (
        lax.all_gather(qkv_weight, "fsdp", axis=1, tiled=True),
        lax.all_gather(query_bias, "fsdp", axis=0, tiled=True),
        lax.all_gather(value_bias, "fsdp", axis=0, tiled=True),
        lax.all_gather(proj_weight, "fsdp", axis=1, tiled=True),
        lax.all_gather(proj_bias, "fsdp", axis=0, tiled=True),
        lax.all_gather(first_gain, "fsdp", axis=0, tiled=True),
        lax.all_gather(first_shift, "fsdp", axis=0, tiled=True),
        lax.all_gather(inner_weight, "fsdp", axis=1, tiled=True),
        lax.all_gather(inner_bias, "fsdp", axis=0, tiled=True),
        lax.all_gather(outer_weight, "fsdp", axis=0, tiled=True),
        lax.all_gather(outer_bias, "fsdp", axis=0, tiled=True),
        lax.all_gather(second_gain, "fsdp", axis=0, tiled=True),
        lax.all_gather(second_shift, "fsdp", axis=0, tiled=True),
        lax.all_gather(embed_table, "fsdp", axis=0, tiled=True),
    )
    chosen = masked_rows[:, None] > 0
    onehot = (replace_ids[:, None] == jnp.arange(TABLE, dtype=jnp.int32)[None, :]).astype(
        jnp.bfloat16
    )
    saved = plain_forward(weights, tokens, chosen, onehot)
    layer_out = plain_norm_rows(
        saved[8], weights[11].astype(jnp.float32), weights[12].astype(jnp.float32)
    ).astype(jnp.bfloat16)
    back_weights = (
        lax.all_gather(qkv_weight, "fsdp", axis=1, tiled=True),
        lax.all_gather(query_bias, "fsdp", axis=0, tiled=True),
        lax.all_gather(value_bias, "fsdp", axis=0, tiled=True),
        lax.all_gather(proj_weight, "fsdp", axis=1, tiled=True),
        lax.all_gather(proj_bias, "fsdp", axis=0, tiled=True),
        lax.all_gather(first_gain, "fsdp", axis=0, tiled=True),
        lax.all_gather(first_shift, "fsdp", axis=0, tiled=True),
        lax.all_gather(inner_weight, "fsdp", axis=1, tiled=True),
        lax.all_gather(inner_bias, "fsdp", axis=0, tiled=True),
        lax.all_gather(outer_weight, "fsdp", axis=0, tiled=True),
        lax.all_gather(outer_bias, "fsdp", axis=0, tiled=True),
        lax.all_gather(second_gain, "fsdp", axis=0, tiled=True),
        lax.all_gather(second_shift, "fsdp", axis=0, tiled=True),
        lax.all_gather(embed_table, "fsdp", axis=0, tiled=True),
    )
    saved = plain_forward(back_weights, tokens, chosen, onehot)
    start_low, qkv_low, logsum, attended, hidden_one, first_low, inner, active, hidden_two = saved
    (
        full_qkv,
        full_query_bias,
        full_value_bias,
        full_proj,
        full_proj_bias,
        full_first_gain,
        full_first_shift,
        full_inner,
        full_inner_bias,
        full_outer,
        full_outer_bias,
        full_second_gain,
        full_second_shift,
        full_table,
    ) = back_weights
    grad_out = jnp.where(chosen, cotangent.astype(jnp.float32), 0.0)
    grad_two, grad_second_gain, grad_second_shift = plain_norm_back(
        hidden_two, full_second_gain, full_second_shift, grad_out
    )
    grad_outer_low = grad_two.astype(jnp.bfloat16)
    grad_outer_bias = jnp.sum(grad_outer_low, axis=0, dtype=jnp.float32)
    grad_outer_weight = jnp.dot(active.T, grad_outer_low, preferred_element_type=jnp.float32)
    grad_active = jnp.dot(grad_outer_low, full_outer.T, preferred_element_type=jnp.float32)
    _, gelu_pull = jax.vjp(partial(jax.nn.gelu, approximate=False), inner)
    grad_inner_low = gelu_pull(grad_active)[0].astype(jnp.bfloat16)
    grad_inner_bias = jnp.sum(grad_inner_low, axis=0, dtype=jnp.float32)
    grad_inner_weight = jnp.dot(first_low.T, grad_inner_low, preferred_element_type=jnp.float32)
    grad_first = grad_two + jnp.dot(
        grad_inner_low, full_inner.T, preferred_element_type=jnp.float32
    )
    grad_one, grad_first_gain, grad_first_shift = plain_norm_back(
        hidden_one, full_first_gain, full_first_shift, grad_first
    )
    grad_proj_low = grad_one.astype(jnp.bfloat16)
    grad_proj_bias = jnp.sum(grad_proj_low, axis=0, dtype=jnp.float32)
    grad_proj_weight = jnp.dot(attended.T, grad_proj_low, preferred_element_type=jnp.float32)
    grad_attended = jnp.dot(grad_proj_low, full_proj.T, preferred_element_type=jnp.float32).astype(
        jnp.bfloat16
    )
    grad_pages = lax.map(
        attend_back,
        (
            qkv_low.reshape(-1, SEQ, 3, HEADS, HEAD),
            logsum,
            grad_attended.reshape(-1, SEQ, HEADS, HEAD),
        ),
    )
    grad_qkv_low = grad_pages.reshape(-1, 3 * D).astype(jnp.bfloat16)
    grad_query_bias = jnp.sum(grad_qkv_low[:, :D], axis=0, dtype=jnp.float32)
    grad_value_bias = jnp.sum(grad_qkv_low[:, 2 * D :], axis=0, dtype=jnp.float32)
    grad_qkv_weight = jnp.dot(start_low.T, grad_qkv_low, preferred_element_type=jnp.float32)
    grad_start = grad_one + jnp.dot(grad_qkv_low, full_qkv.T, preferred_element_type=jnp.float32)
    token_grad = jnp.where(chosen, 0.0, grad_start)
    grad_embed_low = jnp.where(chosen, grad_start, 0.0).astype(jnp.bfloat16)
    grad_table = jnp.dot(onehot.T, grad_embed_low, preferred_element_type=jnp.float32)
    shards = (
        lax.psum_scatter(
            grad_qkv_weight.astype(jnp.bfloat16), "fsdp", scatter_dimension=1, tiled=True
        ).astype(jnp.float32),
        lax.psum_scatter(
            grad_query_bias.astype(jnp.bfloat16), "fsdp", scatter_dimension=0, tiled=True
        ).astype(jnp.float32),
        lax.psum_scatter(
            grad_value_bias.astype(jnp.bfloat16), "fsdp", scatter_dimension=0, tiled=True
        ).astype(jnp.float32),
        lax.psum_scatter(
            grad_proj_weight.astype(jnp.bfloat16), "fsdp", scatter_dimension=1, tiled=True
        ).astype(jnp.float32),
        lax.psum_scatter(
            grad_proj_bias.astype(jnp.bfloat16), "fsdp", scatter_dimension=0, tiled=True
        ).astype(jnp.float32),
        lax.psum_scatter(
            grad_first_gain.astype(jnp.bfloat16), "fsdp", scatter_dimension=0, tiled=True
        ).astype(jnp.float32),
        lax.psum_scatter(
            grad_first_shift.astype(jnp.bfloat16), "fsdp", scatter_dimension=0, tiled=True
        ).astype(jnp.float32),
        lax.psum_scatter(
            grad_inner_weight.astype(jnp.bfloat16), "fsdp", scatter_dimension=1, tiled=True
        ).astype(jnp.float32),
        lax.psum_scatter(
            grad_inner_bias.astype(jnp.bfloat16), "fsdp", scatter_dimension=0, tiled=True
        ).astype(jnp.float32),
        lax.psum_scatter(
            grad_outer_weight.astype(jnp.bfloat16), "fsdp", scatter_dimension=0, tiled=True
        ).astype(jnp.float32),
        lax.psum_scatter(
            grad_outer_bias.astype(jnp.bfloat16), "fsdp", scatter_dimension=0, tiled=True
        ).astype(jnp.float32),
        lax.psum_scatter(
            grad_second_gain.astype(jnp.bfloat16), "fsdp", scatter_dimension=0, tiled=True
        ).astype(jnp.float32),
        lax.psum_scatter(
            grad_second_shift.astype(jnp.bfloat16), "fsdp", scatter_dimension=0, tiled=True
        ).astype(jnp.float32),
        lax.psum_scatter(
            grad_table.astype(jnp.bfloat16), "fsdp", scatter_dimension=0, tiled=True
        ).astype(jnp.float32),
    )
    summed = (
        lax.psum(shards[0].astype(jnp.bfloat16), "dp").astype(jnp.float32),
        lax.psum(shards[1].astype(jnp.bfloat16), "dp").astype(jnp.float32),
        lax.psum(shards[2].astype(jnp.bfloat16), "dp").astype(jnp.float32),
        lax.psum(shards[3].astype(jnp.bfloat16), "dp").astype(jnp.float32),
        lax.psum(shards[4].astype(jnp.bfloat16), "dp").astype(jnp.float32),
        lax.psum(shards[5].astype(jnp.bfloat16), "dp").astype(jnp.float32),
        lax.psum(shards[6].astype(jnp.bfloat16), "dp").astype(jnp.float32),
        lax.psum(shards[7].astype(jnp.bfloat16), "dp").astype(jnp.float32),
        lax.psum(shards[8].astype(jnp.bfloat16), "dp").astype(jnp.float32),
        lax.psum(shards[9].astype(jnp.bfloat16), "dp").astype(jnp.float32),
        lax.psum(shards[10].astype(jnp.bfloat16), "dp").astype(jnp.float32),
        lax.psum(shards[11].astype(jnp.bfloat16), "dp").astype(jnp.float32),
        lax.psum(shards[12].astype(jnp.bfloat16), "dp").astype(jnp.float32),
        lax.psum(shards[13].astype(jnp.bfloat16), "dp").astype(jnp.float32),
    )
    return (
        layer_out,
        token_grad,
        summed[0],
        summed[1],
        summed[2],
        summed[3],
        summed[4],
        summed[5],
        summed[6],
        summed[7],
        summed[8],
        summed[9],
        summed[10],
        summed[11],
        summed[12],
        summed[13],
    )


def solution(mesh):
    direct = mesh.shape["dp"] == 8 and mesh.shape["fsdp"] == 4
    return jax.shard_map(
        local_direct if direct else local_plain,
        mesh=mesh,
        in_specs=(
            P(("dp", "fsdp"), None),
            P(("dp", "fsdp")),
            P(("dp", "fsdp")),
            P(("dp", "fsdp"), None),
            P(None, "fsdp"),
            P("fsdp"),
            P("fsdp"),
            P(None, "fsdp"),
            P("fsdp"),
            P("fsdp"),
            P("fsdp"),
            P(None, "fsdp"),
            P("fsdp"),
            P("fsdp", None),
            P("fsdp"),
            P("fsdp"),
            P("fsdp"),
            P("fsdp", None),
        ),
        out_specs=(
            P(("dp", "fsdp"), None),
            P(("dp", "fsdp"), None),
            P(None, "fsdp"),
            P("fsdp"),
            P("fsdp"),
            P(None, "fsdp"),
            P("fsdp"),
            P("fsdp"),
            P("fsdp"),
            P(None, "fsdp"),
            P("fsdp"),
            P("fsdp", None),
            P("fsdp"),
            P("fsdp"),
            P("fsdp"),
            P("fsdp", None),
        ),
        check_vma=False,
    )
```
